128 devices in a mesh: req: 8 (over y, core), ctx: 16 (over x, z).
Axes of the slice: x: 4, y: 4, z: 4, core: 2. Of those that a mesh axis runs over, the one named last changes fastest.
Arguments:
- queries: bfloat16 [8, 1024, 4096], P('req', 'ctx'), may hold values from -200 to 200
- fresh_kv: bfloat16 [8, 1024, 2048], P('req', 'ctx'), may hold values from -5 to 5
- pool_key_values: bfloat16 [128, 1024, 2048], P(('req', 'ctx')), may hold values from -6 to 6
- holder_map: int32 [128], replicated, may hold values from 0 to 127, each once
- passage_lists: int32 [8, 16], replicated, may hold values from 0 to 127, as said below
- recompute: int32 [8, 1024], P('req'), may hold values from 0 to 16383, as said below
Outputs:
- context: bfloat16 [8, 1024, 4096], P('req', 'ctx')
The draws below stay inside these ranges and needn't reach their ends.
Inputs may be any that keep to these rules, and one draw needn't show every extreme that they name: `passage_lists`: each request names 16 distinct passages. `recompute`: each request lists 1024 distinct positions in rising order; the first is 0 and the last is 16383.
All inputs are finite; a program needn't handle non-finite values.
Results may differ from the reference program's by a relative error of at most 0.0018.
Values may be sent and summed in bfloat16 or wider, within the bound.
No kernel may reach another device: no remote copies, remote signals or barrier semaphores. Data moves between devices by JAX's collectives and lax.ppermute only.
A program may use at most 192 MiB of HBM per device.

```python
import jax
import jax.numpy as jnp
from jax import lax

QUERY_HEADS = 32
KEY_VALUE_HEADS = 8
HEAD_SIZE = 128
PASSAGE_LENGTH = 1024
PASSAGE_COUNT = 16
POOL = 128
REQUEST_COUNT = 8
REDONE_ROWS = 1024


def fresh_base(key):
    return jnp.clip(jax.random.normal(key, (REQUEST_COUNT, REDONE_ROWS, 2 * KEY_VALUE_HEADS * HEAD_SIZE), jnp.float32), -5.0, 5.0)


def draw_queries(key, part):
    key = jax.random.fold_in(key, 11)
    values = jnp.clip(jax.random.normal(key, (REQUEST_COUNT, REDONE_ROWS, QUERY_HEADS * HEAD_SIZE), jnp.float32), -6.0, 6.0)
    return values.astype(jnp.bfloat16)


def draw_fresh_kv(key, part):
    sampled_values = fresh_base(key)
    return sampled_values.astype(jnp.bfloat16)


def draw_pool_key_values(key, part):
    key = jax.random.fold_in(key, 17)
    key_dir, key_mean, key_noise = jax.random.split(key, 3)
    key_span_width = KEY_VALUE_HEADS * HEAD_SIZE
    direction = 0.7 * jax.random.normal(key_dir, (POOL, 1, key_span_width), jnp.float32)
    centre = jax.random.normal(key_mean, (POOL, 1, key_span_width), jnp.float32)
    jitter = jax.random.normal(key_noise, (POOL, PASSAGE_LENGTH, 2 * key_span_width), jnp.float32)
    key_portion = jnp.clip(jitter[:, :, :key_span_width] + direction, -6.0, 6.0)
    values = jnp.clip(0.7 * jitter[:, :, key_span_width:] + centre, -6.0, 6.0)
    return jnp.concatenate([key_portion, values], axis=2).astype(jnp.bfloat16)


def draw_passage_lists(key, part):
    key = jax.random.fold_in(key, 19)
    key_rank, key_noise = jax.random.split(key)
    ranking = jax.random.permutation(key_rank, POOL)
    popular = (ranking < POOL // 16).astype(jnp.int32)
    scores = jax.random.randint(key_noise, (REQUEST_COUNT, POOL), 0, 1024) + 2048 * popular[None, :]
    ranked = scores * POOL + jnp.arange(POOL, dtype=jnp.int32)[None, :]
    chosen = lax.top_k(ranked, PASSAGE_COUNT)[1]
    return chosen.astype(jnp.int32)


def draw_recompute(key, part):
    key = jax.random.fold_in(key, 23)
    key_hot, key_noise = jax.random.split(key)
    heat = jax.random.randint(key_hot, (REQUEST_COUNT, PASSAGE_COUNT), 0, 4)
    warmth = jnp.repeat(heat, PASSAGE_LENGTH, axis=1)
    cell_pos = jnp.arange(PASSAGE_COUNT * PASSAGE_LENGTH, dtype=jnp.int32)
    scores = jax.random.randint(key_noise, (REQUEST_COUNT, PASSAGE_COUNT * PASSAGE_LENGTH), 0, 1024) + 512 * warmth
    forced = ((cell_pos == 0) | (cell_pos == PASSAGE_COUNT * PASSAGE_LENGTH - 1)).astype(jnp.int32) * 4096
    ranked = (scores + forced[None, :]) * (PASSAGE_COUNT * PASSAGE_LENGTH) + cell_pos[None, :]
    chosen = lax.top_k(ranked, REDONE_ROWS)[1]
    return jnp.sort(chosen, axis=1).astype(jnp.int32)


def setup_inputs(seed: int = 0) -> dict:
    key_list = jax.random.split(jax.random.key(seed), 7)
    queries = draw_queries(jax.random.fold_in(key_list[6], 71), 0)
    fresh_kv = draw_fresh_kv(jax.random.fold_in(key_list[6], 71), 0)
    pool_key_values = draw_pool_key_values(jax.random.fold_in(key_list[6], 71), 0)
    holder_map = jax.random.permutation(key_list[3], POOL).astype(jnp.int32)
    passage_lists = draw_passage_lists(jax.random.fold_in(key_list[6], 71), 0)
    recompute = draw_recompute(jax.random.fold_in(key_list[6], 71), 0)
    return {"queries": queries, "fresh_kv": fresh_kv, "pool_key_values": pool_key_values, "holder_map": holder_map, "passage_lists": passage_lists, "recompute": recompute}


MASKED_SCORE = -1e30


def request_context(query_rows, fresh_rows, passage_ids, positions, pool_key_values, holder_map):
    passage_slots = holder_map[passage_ids]
    token_sequence = pool_key_values[passage_slots].reshape(PASSAGE_COUNT * PASSAGE_LENGTH, 2 * KEY_VALUE_HEADS * HEAD_SIZE)
    overall_row_count = positions.shape[0]
    cell_pos = jnp.arange(PASSAGE_COUNT * PASSAGE_LENGTH, dtype=jnp.int32)
    redone = jnp.zeros((PASSAGE_COUNT * PASSAGE_LENGTH,), jnp.int32).at[positions].set(1) > 0
    cached_ok = (cell_pos[None, :] < positions[:, None]) & jnp.logical_not(redone)[None, :]
    cached_ok = cached_ok.reshape(overall_row_count, PASSAGE_COUNT, PASSAGE_LENGTH)
    fresh_ok = positions[None, :] <= positions[:, None]
    key_span_width = KEY_VALUE_HEADS * HEAD_SIZE
    query_group_width = QUERY_HEADS // KEY_VALUE_HEADS
    score_scale = 1.0 / (HEAD_SIZE ** 0.5)

    def each_head_values(head_index):
        query_head = lax.dynamic_slice_in_dim(query_rows, head_index * query_group_width * HEAD_SIZE, query_group_width * HEAD_SIZE, 1)
        query_head = query_head.astype(jnp.float32).reshape(overall_row_count, query_group_width, HEAD_SIZE)
        cached_keys = lax.dynamic_slice_in_dim(token_sequence, head_index * HEAD_SIZE, HEAD_SIZE, 1).astype(jnp.float32)
        cached_values = lax.dynamic_slice_in_dim(token_sequence, key_span_width + head_index * HEAD_SIZE, HEAD_SIZE, 1).astype(jnp.float32)
        cached_keys = cached_keys.reshape(PASSAGE_COUNT, PASSAGE_LENGTH, HEAD_SIZE)
        cached_values = cached_values.reshape(PASSAGE_COUNT, PASSAGE_LENGTH, HEAD_SIZE)
        recomputed_keys = lax.dynamic_slice_in_dim(fresh_rows, head_index * HEAD_SIZE, HEAD_SIZE, 1).astype(jnp.float32)
        recomputed_values = lax.dynamic_slice_in_dim(fresh_rows, key_span_width + head_index * HEAD_SIZE, HEAD_SIZE, 1).astype(jnp.float32)
        cached_scores = jnp.einsum("rgd,pkd->rgpk", query_head, cached_keys) * score_scale
        fresh_scores = jnp.einsum("rgd,kd->rgk", query_head, recomputed_keys) * score_scale
        cached_mask = cached_ok[:, None, :, :]
        cached_masked = jnp.where(cached_mask, cached_scores, MASKED_SCORE)
        fresh_masked = jnp.where(fresh_ok[:, None, :], fresh_scores, MASKED_SCORE)
        block_peak = jnp.max(cached_masked, axis=3)
        fresh_peak = jnp.max(fresh_masked, axis=2)
        cached_weights = jnp.where(cached_mask, jnp.exp(cached_masked - block_peak[..., None]), 0.0)
        fresh_weights = jnp.where(fresh_ok[:, None, :], jnp.exp(fresh_masked - fresh_peak[..., None]), 0.0)
        block_mass = jnp.sum(cached_weights, axis=3)
        fresh_mass = jnp.sum(fresh_weights, axis=2)
        cached_round = lax.optimization_barrier(cached_weights.astype(jnp.bfloat16)).astype(jnp.float32)
        fresh_round = lax.optimization_barrier(fresh_weights.astype(jnp.bfloat16)).astype(jnp.float32)
        block_sum = jnp.einsum("rgpk,pkd->rgpd", cached_round, cached_values)
        fresh_sum = jnp.einsum("rgk,kd->rgd", fresh_round, recomputed_values)
        overall_peak = jnp.maximum(jnp.max(block_peak, axis=2), fresh_peak)
        block_factor = jnp.exp(block_peak - overall_peak[:, :, None])
        fresh_factor = jnp.exp(fresh_peak - overall_peak)
        numerator = jnp.sum(block_sum * block_factor[..., None], axis=2) + fresh_sum * fresh_factor[..., None]
        denominator = jnp.sum(block_mass * block_factor, axis=2) + fresh_mass * fresh_factor
        return numerator / denominator[:, :, None]

    stacked_blocks = lax.map(each_head_values, jnp.arange(KEY_VALUE_HEADS, dtype=jnp.int32))
    return jnp.transpose(stacked_blocks, (1, 0, 2, 3)).reshape(overall_row_count, QUERY_HEADS * HEAD_SIZE).astype(jnp.bfloat16)


def reference(queries, fresh_kv, pool_key_values, holder_map, passage_lists, recompute):
    def one_request(req_index):
        return request_context(queries[req_index], fresh_kv[req_index], passage_lists[req_index],
                               recompute[req_index], pool_key_values, holder_map)

    return lax.map(one_request, jnp.arange(REQUEST_COUNT, dtype=jnp.int32))
```

```python
import functools

import jax
import jax.numpy as jnp
from jax import lax
from jax.experimental import pallas as pl
from jax.experimental.pallas import tpu as pltpu
from jax.sharding import PartitionSpec as P

KEY_VALUE_HEADS = 8
HEAD_SIZE = 128
GROUP = 4
HALVES = 2

MASKED_SCORE = -3e30
FIRST_PEAK = -1e30
NEVER = 1 << 30
LOG2_SCALE = 1.4426950408889634 / HEAD_SIZE**0.5
ROW_BLOCKS = 4
CHUNK = 4
TURNS = ((0, 1), (2, 3), (6, 7), (4, 5))
VMEM_LIMIT = 48 * 1024 * 1024


def pick_kernel(wanted_ref, pieces_ref, *rest):
    outs, sems = rest[:-1], rest[-1]
    count = outs[0].shape[0]
    for d, out in enumerate(outs):
        for j in range(count):
            slot = wanted_ref[d, j]
            pltpu.make_async_copy(pieces_ref.at[slot], out.at[j], sems.at[d]).start()
    for d, out in enumerate(outs):
        pltpu.make_async_copy(out, out, sems.at[d]).wait()


def pick(wanted, pieces):
    turns, count = wanted.shape
    shape = jax.ShapeDtypeStruct((count,) + pieces.shape[1:], pieces.dtype)
    return pl.pallas_call(
        pick_kernel,
        out_shape=[shape] * turns,
        in_specs=[
            pl.BlockSpec(memory_space=pltpu.SMEM),
            pl.BlockSpec(memory_space=pltpu.VMEM),
        ],
        out_specs=[pl.BlockSpec(memory_space=pl.ANY)] * turns,
        scratch_shapes=[pltpu.SemaphoreType.DMA((turns,))],
        compiler_params=pltpu.CompilerParams(vmem_limit_bytes=VMEM_LIMIT),
        cost_estimate=pl.CostEstimate(flops=0, bytes_accessed=2 * pieces.size * 2, transcendentals=0),
        name="pick",
    )(wanted, pieces)


def attend_kernel(piece_count, with_fresh, with_state, last, *refs):
    refs = list(refs)
    scores_ref, peak_ref, mass_ref, sum_ref = refs[-4:]
    refs = refs[:-4]
    steps_ref = refs.pop(0)
    all_ref = refs.pop(0)
    row_ref = refs.pop(0)
    cell_ref = refs.pop(0)
    pieces = [refs.pop(0) for _ in range(piece_count)]
    if with_fresh:
        fresh_cell_ref = refs.pop(0)
    if with_state:
        sum_in, stats_in = refs.pop(0), refs.pop(0)
    blocks, local = row_ref.shape[0], row_ref.shape[1]
    each = GROUP * local
    rows = ROW_BLOCKS * each
    width = scores_ref.shape[2]
    half = (all_ref.shape[1] - each) // 2
    per = width // half

    def fold(values, op):
        folded = values[:, :HEAD_SIZE]
        for n in range(HEAD_SIZE, width, HEAD_SIZE):
            folded = op(folded, values[:, n : n + HEAD_SIZE])
        return folded

    def cached(s, which):
        parts = [piece[pl.ds(s * CHUNK, CHUNK), which] for piece in pieces]
        return jnp.concatenate([part.reshape(-1, HEAD_SIZE) for part in parts], axis=0)

    def fresh(s, which):
        start = each + which * half
        return all_ref[pl.ds(s * per, per), start : start + half, :].reshape(width, HEAD_SIZE)

    def score(first, slot, keys, cells):
        mine = pl.ds(first, ROW_BLOCKS)
        scores = lax.dot_general(
            all_ref[mine, :each, :].reshape(rows, HEAD_SIZE),
            keys,
            (((1,), (1,)), ((), ())),
            preferred_element_type=jnp.float32,
        ).reshape(ROW_BLOCKS, GROUP, local, width)
        row_pos = row_ref[mine]
        usable = jnp.concatenate(
            [cells[None, :, n : n + HEAD_SIZE] < row_pos for n in range(0, width, HEAD_SIZE)],
            axis=2,
        )
        masked = jnp.where(usable[:, None], scores, MASKED_SCORE).reshape(rows, width)
        scores_ref[slot] = masked
        peak_ref[...] = jnp.maximum(peak_ref[...], fold(masked, jnp.maximum))

    def weigh(slot, values):
        peak = peak_ref[...]
        weights = jnp.concatenate(
            [
                jnp.exp2((scores_ref[slot, :, n : n + HEAD_SIZE] - peak) * LOG2_SCALE)
                for n in range(0, width, HEAD_SIZE)
            ],
            axis=1,
        )
        mass_ref[...] += fold(weights, jnp.add)
        sum_ref[...] += jnp.dot(
            weights.astype(jnp.bfloat16), values, preferred_element_type=jnp.float32
        )

    @pl.loop(0, blocks // ROW_BLOCKS)
    def _(block):
        first = block * ROW_BLOCKS
        mine = pl.ds(first, ROW_BLOCKS)
        steps = steps_ref[first + ROW_BLOCKS - 1]
        base = 0
        if with_state:
            old = stats_in[mine].reshape(rows, HEAD_SIZE)
            old_peak, old_mass = old[:, 0:1], old[:, 1:2]
            peak_ref[...] = jnp.broadcast_to(old_peak, peak_ref.shape)
        else:
            peak_ref[...] = jnp.full(peak_ref.shape, FIRST_PEAK, jnp.float32)
        if with_fresh:
            base = blocks // per
            fresh_steps = (first + ROW_BLOCKS - 1) // per + 1

            @pl.loop(0, fresh_steps)
            def _(s):
                score(first, s, fresh(s, 0), fresh_cell_ref[s])

        @pl.loop(0, steps)
        def _(s):
            score(first, base + s, cached(s, 0), cell_ref[s])

        peak = jnp.max(peak_ref[...], axis=1, keepdims=True)
        peak_ref[...] = jnp.broadcast_to(peak, peak_ref.shape)
        mass_ref[...] = jnp.zeros(mass_ref.shape, jnp.float32)
        if with_state:
            keep = jnp.exp2((old_peak - peak) * LOG2_SCALE)
            sum_ref[...] = sum_in[mine].reshape(rows, HEAD_SIZE) * keep
        else:
            sum_ref[...] = jnp.zeros(sum_ref.shape, jnp.float32)
        if with_fresh:

            @pl.loop(0, fresh_steps)
            def _(s):
                weigh(s, fresh(s, 1))

        @pl.loop(0, steps)
        def _(s):
            weigh(base + s, cached(s, 1))

        mass = jnp.sum(mass_ref[...], axis=1, keepdims=True)
        if with_state:
            mass += old_mass * keep
        if not last:
            sum_out, stats_out = refs
            sum_out[mine] = sum_ref[...].reshape(ROW_BLOCKS, each, HEAD_SIZE)
            lane = lax.broadcasted_iota(jnp.int32, (rows, HEAD_SIZE), 1)
            stats = jnp.where(lane == 0, peak, mass)
            stats_out[mine] = stats.reshape(ROW_BLOCKS, each, HEAD_SIZE)
        else:
            (out,) = refs
            out[mine, :each, :] = sum_ref[...].reshape(ROW_BLOCKS, each, HEAD_SIZE)
            eye = lax.broadcasted_iota(jnp.int32, (HEAD_SIZE, HEAD_SIZE), 0)
            eye = eye == lax.broadcasted_iota(jnp.int32, (HEAD_SIZE, HEAD_SIZE), 1)
            for b in range(ROW_BLOCKS):
                lines = []
                for column in (peak, mass):
                    for n in range(b * each, (b + 1) * each, HEAD_SIZE):
                        spread = jnp.where(eye, column[n : n + HEAD_SIZE], 0.0)
                        lines.append(jnp.sum(spread, axis=0, keepdims=True))
                rest = out.shape[1] - each - len(lines)
                lines.append(jnp.zeros((rest, HEAD_SIZE), jnp.float32))
                out[first + b, each:, :] = jnp.concatenate(lines, axis=0)


def attend(steps, gathered, row_pos, cells, pieces, fresh_cells=None, state=None, last=False):
    blocks, local = row_pos.shape[:2]
    rows = GROUP * local
    operands = [steps, gathered, row_pos, cells, *pieces]
    if fresh_cells is not None:
        operands.append(fresh_cells)
    if state is not None:
        operands += list(state)
    in_specs = [pl.BlockSpec(memory_space=pltpu.VMEM)] * len(operands)
    in_specs[0] = pl.BlockSpec(memory_space=pltpu.SMEM)
    if last:
        out_shape = [jax.ShapeDtypeStruct((blocks, rows + 8, HEAD_SIZE), jnp.float32)]
    else:
        out_shape = [jax.ShapeDtypeStruct((blocks, rows, HEAD_SIZE), jnp.float32)] * 2
    width = cells.shape[2]
    slots = cells.shape[0] + (0 if fresh_cells is None else fresh_cells.shape[0])
    keys = slots * width
    tall = ROW_BLOCKS * rows
    return pl.pallas_call(
        functools.partial(
            attend_kernel, len(pieces), fresh_cells is not None, state is not None, last
        ),
        out_shape=out_shape,
        in_specs=in_specs,
        out_specs=[pl.BlockSpec(memory_space=pltpu.VMEM)] * len(out_shape),
        scratch_shapes=[pltpu.VMEM((slots, tall, width), jnp.float32)]
        + [pltpu.VMEM((tall, HEAD_SIZE), jnp.float32)] * 3,
        compiler_params=pltpu.CompilerParams(vmem_limit_bytes=VMEM_LIMIT),
        cost_estimate=pl.CostEstimate(
            flops=2 * 2 * blocks * rows * keys * HEAD_SIZE,
            bytes_accessed=8 * 1024 * 1024,
            transcendentals=blocks * rows * keys,
        ),
        name="attend",
    )(*operands)


def merge_kernel(parts_ref, out_ref):
    local = out_ref.shape[0]
    rows = GROUP * local
    eye = lax.broadcasted_iota(jnp.int32, (HEAD_SIZE, HEAD_SIZE), 0) == lax.broadcasted_iota(
        jnp.int32, (HEAD_SIZE, HEAD_SIZE), 1
    )
    lines = rows // HEAD_SIZE
    peaks = [parts_ref[b, rows : rows + lines, :] for b in range(HALVES)]
    masses = [parts_ref[b, rows + lines : rows + 2 * lines, :] for b in range(HALVES)]
    top = jnp.maximum(peaks[0], peaks[1])
    factors = [jnp.exp2((peak - top) * LOG2_SCALE) for peak in peaks]
    whole = factors[0] * masses[0] + factors[1] * masses[1]
    shares = [factor / whole for factor in factors]
    per_line = HEAD_SIZE // local
    for n in range(lines):
        mixed = 0.0
        for b in range(HALVES):
            column = jnp.sum(jnp.where(eye, shares[b][n : n + 1], 0.0), axis=1, keepdims=True)
            mixed += parts_ref[b, n * HEAD_SIZE : (n + 1) * HEAD_SIZE, :] * column
        mixed = mixed.astype(out_ref.dtype)
        for k in range(per_line):
            g = n * per_line + k
            out_ref[:, g * HEAD_SIZE : (g + 1) * HEAD_SIZE] = mixed[k * local : (k + 1) * local]


def merge(parts, local):
    heads = parts.shape[0] // HALVES
    return pl.pallas_call(
        merge_kernel,
        grid=(heads,),
        out_shape=jax.ShapeDtypeStruct((local, heads * GROUP * HEAD_SIZE), jnp.bfloat16),
        in_specs=[pl.BlockSpec((HALVES,) + parts.shape[1:], lambda h: (h, 0, 0))],
        out_specs=pl.BlockSpec((local, GROUP * HEAD_SIZE), lambda h: (0, h)),
        name="merge",
    )(parts)


def shards(queries, fresh_kv, pool_key_values, holder_map, passage_lists, recompute):
    requests = lax.axis_size("req")
    members = lax.axis_size("ctx")
    me, member = lax.axis_index("req"), lax.axis_index("ctx")
    half = member % HALVES
    length = pool_key_values.shape[1]
    local = queries.shape[1]
    count = passage_lists.shape[1]
    span = length // (requests * HALVES)
    positions = recompute[0]

    pieces = pool_key_values[0].reshape(requests, HALVES, span, 2, KEY_VALUE_HEADS, HEAD_SIZE)
    pieces = pieces.transpose(0, 4, 1, 3, 2, 5).reshape(requests * members, 2, span, HEAD_SIZE)
    with jax.named_scope("scatter_pool"):
        pieces = lax.all_to_all(pieces, ("req", "ctx"), split_axis=0, concat_axis=0, tiled=True)

    query_part = queries[0].reshape(local, KEY_VALUE_HEADS, 1, GROUP, HEAD_SIZE)
    query_part = query_part.transpose(1, 2, 3, 0, 4).reshape(
        KEY_VALUE_HEADS, 1, GROUP * local, HEAD_SIZE
    )
    query_part = jnp.broadcast_to(query_part, (KEY_VALUE_HEADS, HALVES) + query_part.shape[2:])
    fresh_part = fresh_kv[0].reshape(HALVES, local // HALVES, 2, KEY_VALUE_HEADS, HEAD_SIZE)
    fresh_part = fresh_part.transpose(3, 0, 2, 1, 4).reshape(
        KEY_VALUE_HEADS, HALVES, local, HEAD_SIZE
    )
    message = jnp.concatenate([query_part, fresh_part], axis=2)
    message = message.reshape(members, (GROUP + 1) * local, HEAD_SIZE)
    with jax.named_scope("send_queries"):
        gathered = lax.all_to_all(message, "ctx", split_axis=0, concat_axis=0, tiled=True)

    turn = jnp.arange(requests, dtype=jnp.int32) ^ me
    offsets = jnp.arange(span, dtype=jnp.int32)
    cells = (
        jnp.arange(count, dtype=jnp.int32)[None, :, None] * length
        + turn[:, None, None] * (length // requests)
        + half * span
        + offsets[None, None, :]
    )
    redone = jnp.any(cells[..., None] == positions, axis=-1)
    cells = jnp.where(redone, NEVER, cells).reshape(requests, count // CHUNK, CHUNK * span)
    fresh_cells = positions.reshape(members, HALVES, local // HALVES) - 1
    fresh_cells = lax.dynamic_index_in_dim(fresh_cells, half, 1, keepdims=False)
    fresh_cells = fresh_cells.reshape(-1, 1, len(TURNS[0]) * CHUNK * span)
    row_pos = jnp.broadcast_to(positions.reshape(members, local, 1), (members, local, HEAD_SIZE))
    reach = CHUNK * length
    steps = (positions.reshape(members, local)[:, -1] + (reach - 1)) // reach

    wanted = holder_map[passage_lists][turn]
    picked = pick(wanted, pieces)
    with jax.named_scope("send_pieces"):
        arrived = [picked[0]] + [
            lax.ppermute(picked[d], "req", [(i, i ^ d) for i in range(requests)])
            for d in range(1, requests)
        ]

    state = None
    for n, group in enumerate(TURNS):
        place = jnp.concatenate([cells[d] for d in group], axis=1)[:, None, :]
        state = attend(
            steps,
            gathered,
            row_pos,
            place,
            [arrived[d] for d in group],
            fresh_cells if n == 0 else None,
            state,
            n == len(TURNS) - 1,
        )
    with jax.named_scope("send_sums"):
        parts = lax.all_to_all(state[0], "ctx", split_axis=0, concat_axis=0, tiled=True)
    return merge(parts, local)[None]


def solution(mesh):
    in_specs = (
        P("req", "ctx", None),
        P("req", "ctx", None),
        P(("req", "ctx"), None, None),
        P(),
        P(),
        P("req", None),
    )
    out_specs = P("req", "ctx", None)
    return jax.shard_map(shards, mesh=mesh, in_specs=in_specs, out_specs=out_specs, check_vma=False)
```

```python
import functools

import jax
import jax.numpy as jnp
from jax import lax
from jax.experimental import pallas as pl
from jax.experimental.pallas import tpu as pltpu
from jax.sharding import PartitionSpec as P

KEY_VALUE_HEADS = 8
HEAD_SIZE = 128
GROUP = 4
HALVES = 2

MASKED_SCORE = -3e30
FIRST_PEAK = -1e30
NEVER = 1 << 30
LOG2_SCALE = 1.4426950408889634 / HEAD_SIZE**0.5
ROW_BLOCKS = 2
CHUNK = 4
TURNS = ((0, 1), (2, 3), (6, 7), (4, 5))
VMEM_LIMIT = 16 * 1024 * 1024


def cut_kernel(block_ref, out_ref, sem):
    for h in range(KEY_VALUE_HEADS):
        for which in range(2):
            column = (which * KEY_VALUE_HEADS + h) * HEAD_SIZE
            for b in range(HALVES):
                pltpu.make_async_copy(
                    block_ref.at[:, b, :, column : column + HEAD_SIZE],
                    out_ref.at[:, h, b, which],
                    sem,
                ).start()
    pltpu.make_async_copy(out_ref, out_ref, sem).wait()


def cut(block, requests):
    length, wide = block.shape
    span = length // (requests * HALVES)
    pieces = pl.pallas_call(
        cut_kernel,
        out_shape=jax.ShapeDtypeStruct(
            (requests, KEY_VALUE_HEADS, HALVES, 2, span, HEAD_SIZE), block.dtype
        ),
        in_specs=[pl.BlockSpec(memory_space=pl.ANY)],
        out_specs=pl.BlockSpec(memory_space=pl.ANY),
        scratch_shapes=[pltpu.SemaphoreType.DMA],
        compiler_params=pltpu.CompilerParams(vmem_limit_bytes=VMEM_LIMIT),
        name="cut",
    )(block.reshape(requests, HALVES, span, wide))
    return pieces.reshape(-1, 2, span, HEAD_SIZE)


def address_kernel(queries_ref, fresh_ref, out_ref):
    local = queries_ref.shape[0]
    part = local // HALVES
    rows = GROUP * local
    for h in range(KEY_VALUE_HEADS):
        for g in range(GROUP):
            column = (h * GROUP + g) * HEAD_SIZE
            tile = queries_ref[:, column : column + HEAD_SIZE]
            for b in range(HALVES):
                out_ref[h * HALVES + b, g * local : (g + 1) * local, :] = tile
        for which in range(2):
            column = (which * KEY_VALUE_HEADS + h) * HEAD_SIZE
            for b in range(HALVES):
                out_ref[h * HALVES + b, rows + which * part : rows + (which + 1) * part, :] = (
                    fresh_ref[b * part : (b + 1) * part, column : column + HEAD_SIZE]
                )


def address(queries, fresh):
    local = queries.shape[0]
    shape = (KEY_VALUE_HEADS * HALVES, (GROUP + 1) * local, HEAD_SIZE)
    return pl.pallas_call(
        address_kernel,
        out_shape=jax.ShapeDtypeStruct(shape, queries.dtype),
        in_specs=[pl.BlockSpec(memory_space=pltpu.VMEM)] * 2,
        out_specs=pl.BlockSpec(memory_space=pltpu.VMEM),
        name="address",
    )(queries, fresh)


def collect_kernel(parts_ref, queries_ref, fresh_ref):
    rows = parts_ref.shape[1] - fresh_ref.shape[1]
    for c in range(parts_ref.shape[0]):
        queries_ref[:, c * rows : (c + 1) * rows] = parts_ref[c, :rows, :].T
        fresh_ref[c] = parts_ref[c, rows:, :]


def collect(parts, local):
    count, tall = parts.shape[:2]
    rows = GROUP * local
    return pl.pallas_call(
        collect_kernel,
        out_shape=[
            jax.ShapeDtypeStruct((HEAD_SIZE, count * rows), parts.dtype),
            jax.ShapeDtypeStruct((count, tall - rows, HEAD_SIZE), parts.dtype),
        ],
        in_specs=[pl.BlockSpec(memory_space=pltpu.VMEM)],
        out_specs=[pl.BlockSpec(memory_space=pltpu.VMEM)] * 2,
        name="collect",
    )(parts)


def swap(pieces, axis, far):
    return lax.ppermute(pieces, axis, [(i, i ^ far) for i in range(lax.axis_size(axis))])


def pick_kernel(wanted_ref, pieces_ref, *rest):
    outs, sems = rest[:-1], rest[-1]
    count = outs[0].shape[0]
    for d, out in enumerate(outs):
        for j in range(count):
            slot = wanted_ref[d, j]
            pltpu.make_async_copy(pieces_ref.at[slot], out.at[j], sems.at[d]).start()
    for d, out in enumerate(outs):
        pltpu.make_async_copy(out, out, sems.at[d]).wait()


def pick(wanted, pieces):
    turns, count = wanted.shape
    shape = jax.ShapeDtypeStruct((count,) + pieces.shape[1:], pieces.dtype)
    return pl.pallas_call(
        pick_kernel,
        out_shape=[shape] * turns,
        in_specs=[
            pl.BlockSpec(memory_space=pltpu.SMEM),
            pl.BlockSpec(memory_space=pltpu.VMEM),
        ],
        out_specs=[pl.BlockSpec(memory_space=pl.ANY)] * turns,
        scratch_shapes=[pltpu.SemaphoreType.DMA((turns,))],
        compiler_params=pltpu.CompilerParams(vmem_limit_bytes=VMEM_LIMIT),
        cost_estimate=pl.CostEstimate(flops=0, bytes_accessed=2 * pieces.size * 2, transcendentals=0),
        name="pick",
    )(wanted, pieces)


def attend_kernel(piece_count, with_fresh, with_state, last, *refs):
    refs = list(refs)
    pairs_ref, keys_ref, values_ref, *buffers = refs[-9:]
    refs = refs[:-9]
    scores, peaks = buffers[0:2], buffers[2:4]
    if last:
        sum_ref, stats_ref = buffers[4:6]
    steps_ref = refs.pop(0)
    queries_ref = refs.pop(0)
    row_ref = refs.pop(0)
    cell_ref = refs.pop(0)
    pieces = [refs.pop(0) for _ in range(piece_count)]
    if with_fresh:
        fresh_ref = refs.pop(0)
    if with_state:
        sum_in, stats_in = refs.pop(0), refs.pop(0)
    if last:
        (out,) = refs
    else:
        sum_ref, stats_ref = refs
    blocks = steps_ref.shape[0]
    each = queries_ref.shape[1] // blocks
    rows = ROW_BLOCKS * each
    width = keys_ref.shape[1]
    repeats = rows // HEAD_SIZE
    cached_slots = pieces[0].shape[0] // CHUNK
    nothing = cell_ref.shape[0] - 1

    @pl.loop(0, steps_ref[blocks - 1])
    def _(s):
        parts = [piece[pl.ds(s * CHUNK, CHUNK)] for piece in pieces]
        keys_ref[s] = jnp.concatenate([p[:, 0].reshape(-1, HEAD_SIZE) for p in parts], axis=0)
        values_ref[s] = jnp.concatenate([p[:, 1].reshape(-1, HEAD_SIZE) for p in parts], axis=0).T

    keys_ref[nothing] = jnp.zeros(keys_ref.shape[1:], keys_ref.dtype)
    values_ref[nothing] = jnp.zeros(values_ref.shape[1:], values_ref.dtype)
    if with_fresh:
        half = fresh_ref.shape[1] // 2
        per = width // half
        for f in range(blocks // per):
            part = fresh_ref[f * per : (f + 1) * per]
            keys_ref[cached_slots + f] = part[:, :half].reshape(width, HEAD_SIZE)
            values_ref[cached_slots + f] = part[:, half:].reshape(width, HEAD_SIZE).T
    if with_state:
        sum_ref[...] = sum_in[...]
        stats_ref[...] = stats_in[...]
    else:
        sum_ref[...] = jnp.zeros(sum_ref.shape, jnp.float32)
        line = lax.broadcasted_iota(jnp.int32, stats_ref.shape, 0)
        stats_ref[...] = jnp.where(line == 0, FIRST_PEAK, 0.0)

    total = jnp.int32(0)
    for block in range(blocks // ROW_BLOCKS):
        final = (block + 1) * ROW_BLOCKS - 1

        def add(s, total, block=block):
            pairs_ref[0, total] = block
            pairs_ref[1, total] = s
            return total + 1

        total = lax.fori_loop(0, steps_ref[final], add, total)
        if with_fresh:
            total = lax.fori_loop(cached_slots, cached_slots + final // per + 1, add, total)
    for n in range(2):
        pairs_ref[0, total + n] = 0
        pairs_ref[1, total + n] = nothing

    def place(block):
        return pl.ds(pl.multiple_of(block * rows, rows), rows)

    def score(t, side):
        mine, slot = place(pairs_ref[0, t]), pairs_ref[1, t]
        raw = jnp.dot(keys_ref[slot], queries_ref[:, mine], preferred_element_type=jnp.float32)
        usable = jnp.concatenate([cell_ref[slot]] * repeats, axis=1) < row_ref[:, mine]
        masked = jnp.where(usable, raw, MASKED_SCORE)
        scores[side][...] = masked
        peaks[side][...] = jnp.max(masked.reshape(width // 8, 8, rows), axis=0)

    def weigh(t, side):
        mine, slot = place(pairs_ref[0, t]), pairs_ref[1, t]
        old = stats_ref[0:1, mine]
        peak = jnp.maximum(old, jnp.max(peaks[side][...], axis=0, keepdims=True))
        weights = jnp.exp2((scores[side][...] - peak) * LOG2_SCALE)
        keep = jnp.exp2((old - peak) * LOG2_SCALE)
        mass = jnp.sum(weights.reshape(width // 8, 8, rows), axis=0)
        stats_ref[0:1, mine] = peak
        stats_ref[1:2, mine] = stats_ref[1:2, mine] * keep + jnp.sum(mass, axis=0, keepdims=True)
        sum_ref[:, mine] = sum_ref[:, mine] * keep + jnp.dot(
            values_ref[slot], weights.astype(jnp.bfloat16), preferred_element_type=jnp.float32
        )

    score(0, 0)

    @pl.loop(0, (total + 1) // 2)
    def _(u):
        score(2 * u + 1, 1)
        weigh(2 * u, 0)
        score(2 * u + 2, 0)
        weigh(2 * u + 1, 1)

    if last:
        for b in range(blocks):
            part = slice(b * each, (b + 1) * each)
            out[b, :HEAD_SIZE, :] = sum_ref[:, part]
            out[b, HEAD_SIZE:, :] = stats_ref[:, part]


def attend(steps, queries, row_pos, cells, pieces, fresh=None, state=None, last=False):
    blocks, rows = steps.shape[0], queries.shape[1]
    each = rows // blocks
    operands = [steps, queries, row_pos, cells, *pieces]
    if fresh is not None:
        operands.append(fresh)
    if state is not None:
        operands += list(state)
    in_specs = [pl.BlockSpec(memory_space=pltpu.VMEM)] * len(operands)
    in_specs[0] = pl.BlockSpec(memory_space=pltpu.SMEM)
    sums = [(HEAD_SIZE, rows), (8, rows)]
    out_shape = [(blocks, HEAD_SIZE + 8, each)] if last else sums
    slots, width = cells.shape[:2]
    tall = ROW_BLOCKS * each
    keys = slots * width
    return pl.pallas_call(
        functools.partial(attend_kernel, len(pieces), fresh is not None, state is not None, last),
        out_shape=[jax.ShapeDtypeStruct(shape, jnp.float32) for shape in out_shape],
        in_specs=in_specs,
        out_specs=[pl.BlockSpec(memory_space=pltpu.VMEM)] * len(out_shape),
        scratch_shapes=[
            pltpu.SMEM((2, slots * (rows // tall) + 2), jnp.int32),
            pltpu.VMEM((slots, width, HEAD_SIZE), jnp.bfloat16),
            pltpu.VMEM((slots, HEAD_SIZE, width), jnp.bfloat16),
            pltpu.VMEM((width, tall), jnp.float32),
            pltpu.VMEM((width, tall), jnp.float32),
            pltpu.VMEM((8, tall), jnp.float32),
            pltpu.VMEM((8, tall), jnp.float32),
        ]
        + [pltpu.VMEM(shape if last else (8, HEAD_SIZE), jnp.float32) for shape in sums],
        compiler_params=pltpu.CompilerParams(vmem_limit_bytes=VMEM_LIMIT),
        cost_estimate=pl.CostEstimate(
            flops=2 * 2 * rows * keys * HEAD_SIZE,
            bytes_accessed=8 * 1024 * 1024,
            transcendentals=rows * keys,
        ),
        name="attend",
    )(*operands)


def merge_kernel(parts_ref, out_ref):
    local = out_ref.shape[0]
    for h in range(parts_ref.shape[0] // HALVES):
        both = [parts_ref[h * HALVES + b] for b in range(HALVES)]
        peaks = [part[HEAD_SIZE : HEAD_SIZE + 1] for part in both]
        masses = [part[HEAD_SIZE + 1 : HEAD_SIZE + 2] for part in both]
        top = jnp.maximum(peaks[0], peaks[1])
        factors = [jnp.exp2((peak - top) * LOG2_SCALE) for peak in peaks]
        whole = factors[0] * masses[0] + factors[1] * masses[1]
        mixed = sum(
            part[:HEAD_SIZE] * (factor / whole) for part, factor in zip(both, factors)
        ).T.astype(out_ref.dtype)
        for g in range(GROUP):
            place = (h * GROUP + g) * HEAD_SIZE
            out_ref[:, place : place + HEAD_SIZE] = mixed[g * local : (g + 1) * local]


def merge(parts, local):
    heads = parts.shape[0] // HALVES
    return pl.pallas_call(
        merge_kernel,
        out_shape=jax.ShapeDtypeStruct((local, heads * GROUP * HEAD_SIZE), jnp.bfloat16),
        in_specs=[pl.BlockSpec(memory_space=pltpu.VMEM)],
        out_specs=pl.BlockSpec(memory_space=pltpu.VMEM),
        compiler_params=pltpu.CompilerParams(vmem_limit_bytes=VMEM_LIMIT),
        name="merge",
    )(parts)


def spread(column):
    return jnp.broadcast_to(column, column.shape[:-1] + (HEAD_SIZE,))


def shards(queries, fresh_kv, pool_key_values, holder_map, passage_lists, recompute):
    requests = lax.axis_size("req")
    members = lax.axis_size("ctx")
    me, member = lax.axis_index("req"), lax.axis_index("ctx")
    half = member % HALVES
    length = pool_key_values.shape[1]
    local = queries.shape[1]
    count = passage_lists.shape[1]
    span = length // (requests * HALVES)
    positions = recompute[0]

    pieces = cut(pool_key_values[0], requests)
    with jax.named_scope("scatter_pool"):
        pieces = lax.all_to_all(pieces, ("req", "ctx"), split_axis=0, concat_axis=0, tiled=True)
    with jax.named_scope("send_queries"):
        parts = address(queries[0], fresh_kv[0])
        parts = lax.all_to_all(parts, "ctx", split_axis=0, concat_axis=0, tiled=True)
    own_queries, fresh = collect(parts, local)

    turn = jnp.arange(requests, dtype=jnp.int32) ^ me
    offsets = jnp.arange(span, dtype=jnp.int32)
    cells = (
        jnp.arange(count, dtype=jnp.int32)[None, :, None] * length
        + turn[:, None, None] * (length // requests)
        + half * span
        + offsets[None, None, :]
    )
    redone = jnp.any(cells[..., None] == positions, axis=-1)
    cells = jnp.where(redone, NEVER, cells).reshape(requests, count // CHUNK, CHUNK * span, 1)
    fresh_cells = positions.reshape(members, HALVES, local // HALVES) - 1
    fresh_cells = lax.dynamic_index_in_dim(fresh_cells, half, 1, keepdims=False)
    fresh_cells = fresh_cells.reshape(-1, len(TURNS[0]) * CHUNK * span, 1)
    row_pos = jnp.broadcast_to(positions.reshape(members, 1, local), (members, GROUP, local))
    row_pos = row_pos.reshape(1, -1)
    reach = CHUNK * length
    steps = (positions.reshape(members, local)[:, -1] + (reach - 1)) // reach

    wanted = holder_map[passage_lists][turn]
    picked = pick(wanted, pieces)
    with jax.named_scope("send_pieces"):
        arrived = {0: picked[0]}
        for d in (2, 3, 6, 7, 1):
            arrived[d] = swap(picked[d], "req", d)
        arrived[2], arrived[3], *far = lax.optimization_barrier(
            (arrived[2], arrived[3], picked[4], picked[5])
        )
        arrived[4], arrived[5] = swap(far[0], "req", 4), swap(far[1], "req", 5)

    nothing = jnp.full((1,) + fresh_cells.shape[1:], NEVER, jnp.int32)
    state = None
    for n, group in enumerate(TURNS):
        place = [jnp.concatenate([cells[d] for d in group], axis=1)]
        if n == 0:
            place.append(fresh_cells)
        place.append(nothing[:, : place[0].shape[1]])
        state = attend(
            steps,
            own_queries,
            row_pos,
            spread(jnp.concatenate(place, axis=0)),
            [arrived[d] for d in group],
            fresh if n == 0 else None,
            state,
            n == len(TURNS) - 1,
        )
    with jax.named_scope("send_sums"):
        parts = lax.all_to_all(state[0], "ctx", split_axis=0, concat_axis=0, tiled=True)
    return merge(parts, local)[None]


def solution(mesh):
    in_specs = (
        P("req", "ctx", None),
        P("req", "ctx", None),
        P(("req", "ctx"), None, None),
        P(),
        P(),
        P("req", None),
    )
    out_specs = P("req", "ctx", None)
    return jax.shard_map(shards, mesh=mesh, in_specs=in_specs, out_specs=out_specs, check_vma=False)
```

```python
import functools

import jax
import jax.numpy as jnp
from jax import lax
from jax.experimental import pallas as pl
from jax.experimental.pallas import tpu as pltpu
from jax.sharding import PartitionSpec as P

KEY_VALUE_HEADS = 8
HEAD_SIZE = 128
GROUP = 4
HALVES = 2

MASKED_SCORE = -3e30
FIRST_PEAK = -1e30
NEVER = 1 << 30
LOG2_SCALE = 1.4426950408889634 / HEAD_SIZE**0.5
ROW_BLOCKS = 2
CHUNK = 4
TURNS = ((0, 1), (2, 3), (6, 7), (4, 5))
VMEM_LIMIT = 16 * 1024 * 1024


def cut_kernel(block_ref, out_ref, sem):
    for h in range(KEY_VALUE_HEADS):
        for which in range(2):
            column = (which * KEY_VALUE_HEADS + h) * HEAD_SIZE
            for b in range(HALVES):
                pltpu.make_async_copy(
                    block_ref.at[:, b, :, column : column + HEAD_SIZE],
                    out_ref.at[:, h, b, which],
                    sem,
                ).start()
    pltpu.make_async_copy(out_ref, out_ref, sem).wait()


def cut(block, requests):
    length, wide = block.shape
    span = length // (requests * HALVES)
    pieces = pl.pallas_call(
        cut_kernel,
        out_shape=jax.ShapeDtypeStruct(
            (requests, KEY_VALUE_HEADS, HALVES, 2, span, HEAD_SIZE), block.dtype
        ),
        in_specs=[pl.BlockSpec(memory_space=pl.ANY)],
        out_specs=pl.BlockSpec(memory_space=pl.ANY),
        scratch_shapes=[pltpu.SemaphoreType.DMA],
        compiler_params=pltpu.CompilerParams(vmem_limit_bytes=VMEM_LIMIT),
        name="cut",
    )(block.reshape(requests, HALVES, span, wide))
    return pieces.reshape(-1, 2, span, HEAD_SIZE)


def address_kernel(queries_ref, fresh_ref, out_ref):
    local = queries_ref.shape[0]
    part = local // HALVES
    rows = GROUP * local
    for h in range(KEY_VALUE_HEADS):
        for g in range(GROUP):
            column = (h * GROUP + g) * HEAD_SIZE
            tile = queries_ref[:, column : column + HEAD_SIZE]
            for b in range(HALVES):
                out_ref[h * HALVES + b, g * local : (g + 1) * local, :] = tile
        for which in range(2):
            column = (which * KEY_VALUE_HEADS + h) * HEAD_SIZE
            for b in range(HALVES):
                out_ref[h * HALVES + b, rows + which * part : rows + (which + 1) * part, :] = (
                    fresh_ref[b * part : (b + 1) * part, column : column + HEAD_SIZE]
                )


def address(queries, fresh):
    local = queries.shape[0]
    shape = (KEY_VALUE_HEADS * HALVES, (GROUP + 1) * local, HEAD_SIZE)
    return pl.pallas_call(
        address_kernel,
        out_shape=jax.ShapeDtypeStruct(shape, queries.dtype),
        in_specs=[pl.BlockSpec(memory_space=pltpu.VMEM)] * 2,
        out_specs=pl.BlockSpec(memory_space=pltpu.VMEM),
        name="address",
    )(queries, fresh)


def collect_kernel(parts_ref, queries_ref, fresh_ref):
    rows = parts_ref.shape[1] - fresh_ref.shape[1]
    for c in range(parts_ref.shape[0]):
        queries_ref[:, c * rows : (c + 1) * rows] = parts_ref[c, :rows, :].T
        fresh_ref[c] = parts_ref[c, rows:, :]


def collect(parts, local):
    count, tall = parts.shape[:2]
    rows = GROUP * local
    return pl.pallas_call(
        collect_kernel,
        out_shape=[
            jax.ShapeDtypeStruct((HEAD_SIZE, count * rows), parts.dtype),
            jax.ShapeDtypeStruct((count, tall - rows, HEAD_SIZE), parts.dtype),
        ],
        in_specs=[pl.BlockSpec(memory_space=pltpu.VMEM)],
        out_specs=[pl.BlockSpec(memory_space=pltpu.VMEM)] * 2,
        name="collect",
    )(parts)


def swap(pieces, axis, far):
    return lax.ppermute(pieces, axis, [(i, i ^ far) for i in range(lax.axis_size(axis))])


def pick_kernel(wanted_ref, pieces_ref, *rest):
    outs, sems = rest[:-1], rest[-1]
    count = outs[0].shape[0]
    for d, out in enumerate(outs):
        for j in range(count):
            slot = wanted_ref[d, j]
            pltpu.make_async_copy(pieces_ref.at[slot], out.at[j], sems.at[d]).start()
    for d, out in enumerate(outs):
        pltpu.make_async_copy(out, out, sems.at[d]).wait()


def pick(wanted, pieces):
    turns, count = wanted.shape
    shape = jax.ShapeDtypeStruct((count,) + pieces.shape[1:], pieces.dtype)
    return pl.pallas_call(
        pick_kernel,
        out_shape=[shape] * turns,
        in_specs=[
            pl.BlockSpec(memory_space=pltpu.SMEM),
            pl.BlockSpec(memory_space=pltpu.VMEM),
        ],
        out_specs=[pl.BlockSpec(memory_space=pl.ANY)] * turns,
        scratch_shapes=[pltpu.SemaphoreType.DMA((turns,))],
        compiler_params=pltpu.CompilerParams(vmem_limit_bytes=VMEM_LIMIT),
        cost_estimate=pl.CostEstimate(flops=0, bytes_accessed=2 * pieces.size * 2, transcendentals=0),
        name="pick",
    )(wanted, pieces)


def attend_kernel(piece_count, with_fresh, with_state, last, *refs):
    refs = list(refs)
    pairs_ref, keys_ref, values_ref, *buffers = refs[-9:]
    refs = refs[:-9]
    scores, peaks = buffers[0:2], buffers[2:4]
    if last:
        sum_ref, stats_ref = buffers[4:6]
    steps_ref = refs.pop(0)
    queries_ref = refs.pop(0)
    row_ref = refs.pop(0)
    cell_ref = refs.pop(0)
    pieces = [refs.pop(0) for _ in range(piece_count)]
    if with_fresh:
        fresh_ref = refs.pop(0)
    if with_state:
        sum_in, stats_in = refs.pop(0), refs.pop(0)
    if last:
        (out,) = refs
    else:
        sum_ref, stats_ref = refs
    blocks = steps_ref.shape[0]
    each = queries_ref.shape[1] // blocks
    rows = ROW_BLOCKS * each
    width = keys_ref.shape[1]
    repeats = rows // HEAD_SIZE
    cached_slots = pieces[0].shape[0] // CHUNK
    nothing = cell_ref.shape[0] - 1

    @pl.loop(0, steps_ref[blocks - 1])
    def _(s):
        parts = [piece[pl.ds(s * CHUNK, CHUNK)] for piece in pieces]
        keys_ref[s] = jnp.concatenate([p[:, 0].reshape(-1, HEAD_SIZE) for p in parts], axis=0)
        values_ref[s] = jnp.concatenate([p[:, 1].reshape(-1, HEAD_SIZE) for p in parts], axis=0).T

    keys_ref[nothing] = jnp.zeros(keys_ref.shape[1:], keys_ref.dtype)
    values_ref[nothing] = jnp.zeros(values_ref.shape[1:], values_ref.dtype)
    if with_fresh:
        half = fresh_ref.shape[1] // 2
        per = width // half
        for f in range(blocks // per):
            part = fresh_ref[f * per : (f + 1) * per]
            keys_ref[cached_slots + f] = part[:, :half].reshape(width, HEAD_SIZE)
            values_ref[cached_slots + f] = part[:, half:].reshape(width, HEAD_SIZE).T
    if with_state:
        sum_ref[...] = sum_in[...]
        stats_ref[...] = stats_in[...]
    else:
        sum_ref[...] = jnp.zeros(sum_ref.shape, jnp.float32)
        line = lax.broadcasted_iota(jnp.int32, stats_ref.shape, 0)
        stats_ref[...] = jnp.where(line == 0, FIRST_PEAK, 0.0)

    total = jnp.int32(0)
    for block in range(blocks // ROW_BLOCKS):
        final = (block + 1) * ROW_BLOCKS - 1

        def add(s, total, block=block):
            pairs_ref[0, total] = block
            pairs_ref[1, total] = s
            return total + 1

        total = lax.fori_loop(0, steps_ref[final], add, total)
        if with_fresh:
            total = lax.fori_loop(cached_slots, cached_slots + final // per + 1, add, total)
    for n in range(2):
        pairs_ref[0, total + n] = 0
        pairs_ref[1, total + n] = nothing

    def place(block):
        return pl.ds(pl.multiple_of(block * rows, rows), rows)

    def score(t, side):
        mine, slot = place(pairs_ref[0, t]), pairs_ref[1, t]
        raw = jnp.dot(keys_ref[slot], queries_ref[:, mine], preferred_element_type=jnp.float32)
        usable = jnp.concatenate([cell_ref[slot]] * repeats, axis=1) < row_ref[:, mine]
        masked = jnp.where(usable, raw, MASKED_SCORE)
        scores[side][...] = masked
        peaks[side][...] = jnp.max(masked.reshape(width // 8, 8, rows), axis=0)

    def weigh(t, side):
        mine, slot = place(pairs_ref[0, t]), pairs_ref[1, t]
        old = stats_ref[0:1, mine]
        peak = jnp.maximum(old, jnp.max(peaks[side][...], axis=0, keepdims=True))
        weights = jnp.exp2((scores[side][...] - peak) * LOG2_SCALE)
        keep = jnp.exp2((old - peak) * LOG2_SCALE)
        mass = jnp.sum(weights.reshape(width // 8, 8, rows), axis=0)
        stats_ref[0:1, mine] = peak
        stats_ref[1:2, mine] = stats_ref[1:2, mine] * keep + jnp.sum(mass, axis=0, keepdims=True)
        sum_ref[:, mine] = sum_ref[:, mine] * keep + jnp.dot(
            values_ref[slot], weights.astype(jnp.bfloat16), preferred_element_type=jnp.float32
        )

    score(0, 0)

    @pl.loop(0, (total + 1) // 2)
    def _(u):
        score(2 * u + 1, 1)
        weigh(2 * u, 0)
        score(2 * u + 2, 0)
        weigh(2 * u + 1, 1)

    if last:
        for b in range(blocks):
            part = slice(b * each, (b + 1) * each)
            out[b, :HEAD_SIZE, :] = sum_ref[:, part]
            out[b, HEAD_SIZE:, :] = stats_ref[:, part]


def attend(steps, queries, row_pos, cells, pieces, fresh=None, state=None, last=False):
    blocks, rows = steps.shape[0], queries.shape[1]
    each = rows // blocks
    operands = [steps, queries, row_pos, cells, *pieces]
    if fresh is not None:
        operands.append(fresh)
    if state is not None:
        operands += list(state)
    in_specs = [pl.BlockSpec(memory_space=pltpu.VMEM)] * len(operands)
    in_specs[0] = pl.BlockSpec(memory_space=pltpu.SMEM)
    sums = [(HEAD_SIZE, rows), (8, rows)]
    out_shape = [(blocks, HEAD_SIZE + 8, each)] if last else sums
    slots, width = cells.shape[:2]
    tall = ROW_BLOCKS * each
    keys = slots * width
    return pl.pallas_call(
        functools.partial(attend_kernel, len(pieces), fresh is not None, state is not None, last),
        out_shape=[jax.ShapeDtypeStruct(shape, jnp.float32) for shape in out_shape],
        in_specs=in_specs,
        out_specs=[pl.BlockSpec(memory_space=pltpu.VMEM)] * len(out_shape),
        scratch_shapes=[
            pltpu.SMEM((2, slots * (rows // tall) + 2), jnp.int32),
            pltpu.VMEM((slots, width, HEAD_SIZE), jnp.bfloat16),
            pltpu.VMEM((slots, HEAD_SIZE, width), jnp.bfloat16),
            pltpu.VMEM((width, tall), jnp.float32),
            pltpu.VMEM((width, tall), jnp.float32),
            pltpu.VMEM((8, tall), jnp.float32),
            pltpu.VMEM((8, tall), jnp.float32),
        ]
        + [pltpu.VMEM(shape if last else (8, HEAD_SIZE), jnp.float32) for shape in sums],
        compiler_params=pltpu.CompilerParams(vmem_limit_bytes=VMEM_LIMIT),
        cost_estimate=pl.CostEstimate(
            flops=2 * 2 * rows * keys * HEAD_SIZE,
            bytes_accessed=8 * 1024 * 1024,
            transcendentals=rows * keys,
        ),
        name="attend",
    )(*operands)


def merge_kernel(parts_ref, out_ref):
    local = out_ref.shape[0]
    for h in range(parts_ref.shape[0] // HALVES):
        both = [parts_ref[h * HALVES + b] for b in range(HALVES)]
        peaks = [part[HEAD_SIZE : HEAD_SIZE + 1] for part in both]
        masses = [part[HEAD_SIZE + 1 : HEAD_SIZE + 2] for part in both]
        top = jnp.maximum(peaks[0], peaks[1])
        factors = [jnp.exp2((peak - top) * LOG2_SCALE) for peak in peaks]
        whole = factors[0] * masses[0] + factors[1] * masses[1]
        mixed = sum(
            part[:HEAD_SIZE] * (factor / whole) for part, factor in zip(both, factors)
        ).T.astype(out_ref.dtype)
        for g in range(GROUP):
            place = (h * GROUP + g) * HEAD_SIZE
            out_ref[:, place : place + HEAD_SIZE] = mixed[g * local : (g + 1) * local]


def merge(parts, local):
    heads = parts.shape[0] // HALVES
    return pl.pallas_call(
        merge_kernel,
        out_shape=jax.ShapeDtypeStruct((local, heads * GROUP * HEAD_SIZE), jnp.bfloat16),
        in_specs=[pl.BlockSpec(memory_space=pltpu.VMEM)],
        out_specs=pl.BlockSpec(memory_space=pltpu.VMEM),
        compiler_params=pltpu.CompilerParams(vmem_limit_bytes=VMEM_LIMIT),
        name="merge",
    )(parts)


def spread(column):
    return jnp.broadcast_to(column, column.shape[:-1] + (HEAD_SIZE,))


def shards(queries, fresh_kv, pool_key_values, holder_map, passage_lists, recompute):
    requests = lax.axis_size("req")
    members = lax.axis_size("ctx")
    me, member = lax.axis_index("req"), lax.axis_index("ctx")
    half = member % HALVES
    length = pool_key_values.shape[1]
    local = queries.shape[1]
    count = passage_lists.shape[1]
    span = length // (requests * HALVES)
    positions = recompute[0]

    pieces = cut(pool_key_values[0], requests)
    with jax.named_scope("scatter_pool"):
        pieces = lax.all_to_all(pieces, ("req", "ctx"), split_axis=0, concat_axis=0, tiled=True)
    with jax.named_scope("send_queries"):
        parts = address(queries[0], fresh_kv[0])
        parts = lax.all_to_all(parts, "ctx", split_axis=0, concat_axis=0, tiled=True)
    own_queries, fresh = collect(parts, local)

    turn = jnp.arange(requests, dtype=jnp.int32) ^ me
    offsets = jnp.arange(span, dtype=jnp.int32)
    cells = (
        jnp.arange(count, dtype=jnp.int32)[None, :, None] * length
        + turn[:, None, None] * (length // requests)
        + half * span
        + offsets[None, None, :]
    )
    redone = jnp.any(cells[..., None] == positions, axis=-1)
    cells = jnp.where(redone, NEVER, cells).reshape(requests, count // CHUNK, CHUNK * span, 1)
    fresh_cells = positions.reshape(members, HALVES, local // HALVES) - 1
    fresh_cells = lax.dynamic_index_in_dim(fresh_cells, half, 1, keepdims=False)
    fresh_cells = fresh_cells.reshape(-1, len(TURNS[0]) * CHUNK * span, 1)
    row_pos = jnp.broadcast_to(positions.reshape(members, 1, local), (members, GROUP, local))
    row_pos = row_pos.reshape(1, -1)
    reach = CHUNK * length
    steps = (positions.reshape(members, local)[:, -1] + (reach - 1)) // reach

    wanted = holder_map[passage_lists][turn]
    picked = pick(wanted, pieces)
    with jax.named_scope("send_pieces"):
        arrived = {0: picked[0]}
        for d in (2, 3, 6, 7, 1):
            arrived[d] = swap(picked[d], "req", d)

    nothing = jnp.full((1,) + fresh_cells.shape[1:], NEVER, jnp.int32)
    state = None
    for n, group in enumerate(TURNS):
        place = [jnp.concatenate([cells[d] for d in group], axis=1)]
        if n == 0:
            place.append(fresh_cells)
        place.append(nothing[:, : place[0].shape[1]])
        state = attend(
            steps,
            own_queries,
            row_pos,
            spread(jnp.concatenate(place, axis=0)),
            [arrived[d] for d in group],
            fresh if n == 0 else None,
            state,
            n == len(TURNS) - 1,
        )
        if n == 0:
            *state, far, farther = lax.optimization_barrier((*state, picked[4], picked[5]))
            with jax.named_scope("send_pieces"):
                arrived[4], arrived[5] = swap(far, "req", 4), swap(farther, "req", 5)
    with jax.named_scope("send_sums"):
        parts = lax.all_to_all(state[0], "ctx", split_axis=0, concat_axis=0, tiled=True)
    return merge(parts, local)[None]


def solution(mesh):
    in_specs = (
        P("req", "ctx", None),
        P("req", "ctx", None),
        P(("req", "ctx"), None, None),
        P(),
        P(),
        P("req", None),
    )
    out_specs = P("req", "ctx", None)
    return jax.shard_map(shards, mesh=mesh, in_specs=in_specs, out_specs=out_specs, check_vma=False)
```

```python
import functools

import jax
import jax.numpy as jnp
from jax import lax
from jax.experimental import pallas as pl
from jax.experimental.pallas import tpu as pltpu
from jax.sharding import PartitionSpec as P

KEY_VALUE_HEADS = 8
HEAD_SIZE = 128
GROUP = 4
HALVES = 2

MASKED_SCORE = -3e30
FIRST_PEAK = -1e30
NEVER = 1 << 30
LOG2_SCALE = 1.4426950408889634 / HEAD_SIZE**0.5
ROW_BLOCKS = 2
CHUNK = 4
TURNS = ((0, 1), (2, 3), (6, 7), (4, 5))
VMEM_LIMIT = 16 * 1024 * 1024


def cut_kernel(block_ref, out_ref, sem):
    for h in range(KEY_VALUE_HEADS):
        for which in range(2):
            column = (which * KEY_VALUE_HEADS + h) * HEAD_SIZE
            for b in range(HALVES):
                pltpu.make_async_copy(
                    block_ref.at[:, b, :, column : column + HEAD_SIZE],
                    out_ref.at[:, h, b, which],
                    sem,
                ).start()
    pltpu.make_async_copy(out_ref, out_ref, sem).wait()


def cut(block, requests):
    length, wide = block.shape
    span = length // (requests * HALVES)
    pieces = pl.pallas_call(
        cut_kernel,
        out_shape=jax.ShapeDtypeStruct(
            (requests, KEY_VALUE_HEADS, HALVES, 2, span, HEAD_SIZE), block.dtype
        ),
        in_specs=[pl.BlockSpec(memory_space=pl.ANY)],
        out_specs=pl.BlockSpec(memory_space=pl.ANY),
        scratch_shapes=[pltpu.SemaphoreType.DMA],
        compiler_params=pltpu.CompilerParams(vmem_limit_bytes=VMEM_LIMIT),
        name="cut",
    )(block.reshape(requests, HALVES, span, wide))
    return pieces.reshape(-1, 2, span, HEAD_SIZE)


def address_kernel(queries_ref, fresh_ref, out_ref):
    local = queries_ref.shape[0]
    part = local // HALVES
    rows = GROUP * local
    for h in range(KEY_VALUE_HEADS):
        for g in range(GROUP):
            column = (h * GROUP + g) * HEAD_SIZE
            tile = queries_ref[:, column : column + HEAD_SIZE]
            for b in range(HALVES):
                out_ref[h * HALVES + b, g * local : (g + 1) * local, :] = tile
        for which in range(2):
            column = (which * KEY_VALUE_HEADS + h) * HEAD_SIZE
            for b in range(HALVES):
                out_ref[h * HALVES + b, rows + which * part : rows + (which + 1) * part, :] = (
                    fresh_ref[b * part : (b + 1) * part, column : column + HEAD_SIZE]
                )


def address(queries, fresh):
    local = queries.shape[0]
    shape = (KEY_VALUE_HEADS * HALVES, (GROUP + 1) * local, HEAD_SIZE)
    return pl.pallas_call(
        address_kernel,
        out_shape=jax.ShapeDtypeStruct(shape, queries.dtype),
        in_specs=[pl.BlockSpec(memory_space=pltpu.VMEM)] * 2,
        out_specs=pl.BlockSpec(memory_space=pltpu.VMEM),
        name="address",
    )(queries, fresh)


def collect_kernel(parts_ref, queries_ref, fresh_ref):
    rows = parts_ref.shape[1] - fresh_ref.shape[1]
    for c in range(parts_ref.shape[0]):
        queries_ref[:, c * rows : (c + 1) * rows] = parts_ref[c, :rows, :].T
        fresh_ref[c] = parts_ref[c, rows:, :]


def collect(parts, local):
    count, tall = parts.shape[:2]
    rows = GROUP * local
    return pl.pallas_call(
        collect_kernel,
        out_shape=[
            jax.ShapeDtypeStruct((HEAD_SIZE, count * rows), parts.dtype),
            jax.ShapeDtypeStruct((count, tall - rows, HEAD_SIZE), parts.dtype),
        ],
        in_specs=[pl.BlockSpec(memory_space=pltpu.VMEM)],
        out_specs=[pl.BlockSpec(memory_space=pltpu.VMEM)] * 2,
        name="collect",
    )(parts)


def swap(pieces, axis, far):
    return lax.ppermute(pieces, axis, [(i, i ^ far) for i in range(lax.axis_size(axis))])


def pick_kernel(wanted_ref, pieces_ref, *rest):
    outs, sems = rest[:-1], rest[-1]
    count = outs[0].shape[0]
    for d, out in enumerate(outs):
        for j in range(count):
            slot = wanted_ref[d, j]
            pltpu.make_async_copy(pieces_ref.at[slot], out.at[j], sems.at[d]).start()
    for d, out in enumerate(outs):
        pltpu.make_async_copy(out, out, sems.at[d]).wait()


def pick(wanted, pieces):
    turns, count = wanted.shape
    shape = jax.ShapeDtypeStruct((count,) + pieces.shape[1:], pieces.dtype)
    return pl.pallas_call(
        pick_kernel,
        out_shape=[shape] * turns,
        in_specs=[
            pl.BlockSpec(memory_space=pltpu.SMEM),
            pl.BlockSpec(memory_space=pltpu.VMEM),
        ],
        out_specs=[pl.BlockSpec(memory_space=pl.ANY)] * turns,
        scratch_shapes=[pltpu.SemaphoreType.DMA((turns,))],
        compiler_params=pltpu.CompilerParams(vmem_limit_bytes=VMEM_LIMIT),
        cost_estimate=pl.CostEstimate(flops=0, bytes_accessed=2 * pieces.size * 2, transcendentals=0),
        name="pick",
    )(wanted, pieces)


def attend_kernel(piece_count, with_fresh, with_state, last, *refs):
    refs = list(refs)
    pairs_ref, keys_ref, values_ref, *buffers = refs[-9:]
    refs = refs[:-9]
    scores, peaks = buffers[0:2], buffers[2:4]
    if last:
        sum_ref, stats_ref = buffers[4:6]
    steps_ref = refs.pop(0)
    queries_ref = refs.pop(0)
    row_ref = refs.pop(0)
    cell_ref = refs.pop(0)
    pieces = [refs.pop(0) for _ in range(piece_count)]
    if with_fresh:
        fresh_ref = refs.pop(0)
    if with_state:
        sum_in, stats_in = refs.pop(0), refs.pop(0)
    if last:
        (out,) = refs
    else:
        sum_ref, stats_ref = refs
    blocks = steps_ref.shape[0]
    each = queries_ref.shape[1] // blocks
    rows = ROW_BLOCKS * each
    width = keys_ref.shape[1]
    repeats = rows // HEAD_SIZE
    cached_slots = pieces[0].shape[0] // CHUNK if pieces else 0
    nothing = cell_ref.shape[0] - 1

    if pieces:

        @pl.loop(0, steps_ref[blocks - 1])
        def _(s):
            parts = [piece[pl.ds(s * CHUNK, CHUNK)] for piece in pieces]
            for which, ref in ((0, keys_ref), (1, values_ref)):
                lines = [part[:, which].reshape(-1, HEAD_SIZE) for part in parts]
                lines = jnp.concatenate(lines, axis=0)
                ref[s] = lines.T if which else lines

    keys_ref[nothing] = jnp.zeros(keys_ref.shape[1:], keys_ref.dtype)
    values_ref[nothing] = jnp.zeros(values_ref.shape[1:], values_ref.dtype)
    if with_fresh:
        half = fresh_ref.shape[1] // 2
        per = width // half
        for f in range(blocks // per):
            part = fresh_ref[f * per : (f + 1) * per]
            keys_ref[cached_slots + f] = part[:, :half].reshape(width, HEAD_SIZE)
            values_ref[cached_slots + f] = part[:, half:].reshape(width, HEAD_SIZE).T
    if with_state:
        sum_ref[...] = sum_in[...]
        stats_ref[...] = stats_in[...]
    else:
        sum_ref[...] = jnp.zeros(sum_ref.shape, jnp.float32)
        line = lax.broadcasted_iota(jnp.int32, stats_ref.shape, 0)
        stats_ref[...] = jnp.where(line == 0, FIRST_PEAK, 0.0)

    total = jnp.int32(0)
    for block in range(blocks // ROW_BLOCKS):
        final = (block + 1) * ROW_BLOCKS - 1

        def add(s, total, block=block):
            pairs_ref[0, total] = block
            pairs_ref[1, total] = s
            return total + 1

        if pieces:
            total = lax.fori_loop(0, steps_ref[final], add, total)
        if with_fresh:
            total = lax.fori_loop(cached_slots, cached_slots + final // per + 1, add, total)
    for n in range(2):
        pairs_ref[0, total + n] = 0
        pairs_ref[1, total + n] = nothing

    def place(block):
        return pl.ds(pl.multiple_of(block * rows, rows), rows)

    def score(t, side):
        mine, slot = place(pairs_ref[0, t]), pairs_ref[1, t]
        raw = jnp.dot(keys_ref[slot], queries_ref[:, mine], preferred_element_type=jnp.float32)
        usable = jnp.concatenate([cell_ref[slot]] * repeats, axis=1) < row_ref[:, mine]
        masked = jnp.where(usable, raw, MASKED_SCORE)
        scores[side][...] = masked
        peaks[side][...] = jnp.max(masked.reshape(width // 8, 8, rows), axis=0)

    def weigh(t, side):
        mine, slot = place(pairs_ref[0, t]), pairs_ref[1, t]
        old = stats_ref[0:1, mine]
        peak = jnp.maximum(old, jnp.max(peaks[side][...], axis=0, keepdims=True))
        weights = jnp.exp2((scores[side][...] - peak) * LOG2_SCALE)
        keep = jnp.exp2((old - peak) * LOG2_SCALE)
        mass = jnp.sum(weights.reshape(width // 8, 8, rows), axis=0)
        stats_ref[0:1, mine] = peak
        stats_ref[1:2, mine] = stats_ref[1:2, mine] * keep + jnp.sum(mass, axis=0, keepdims=True)
        sum_ref[:, mine] = sum_ref[:, mine] * keep + jnp.dot(
            values_ref[slot], weights.astype(jnp.bfloat16), preferred_element_type=jnp.float32
        )

    score(0, 0)

    @pl.loop(0, (total + 1) // 2)
    def _(u):
        score(2 * u + 1, 1)
        weigh(2 * u, 0)
        score(2 * u + 2, 0)
        weigh(2 * u + 1, 1)

    if last:
        for b in range(blocks):
            part = slice(b * each, (b + 1) * each)
            out[b, :HEAD_SIZE, :] = sum_ref[:, part]
            out[b, HEAD_SIZE:, :] = stats_ref[:, part]


def attend(steps, queries, row_pos, cells, pieces, fresh=None, state=None, last=False):
    blocks, rows = steps.shape[0], queries.shape[1]
    each = rows // blocks
    operands = [steps, queries, row_pos, cells, *pieces]
    if fresh is not None:
        operands.append(fresh)
    if state is not None:
        operands += list(state)
    in_specs = [pl.BlockSpec(memory_space=pltpu.VMEM)] * len(operands)
    in_specs[0] = pl.BlockSpec(memory_space=pltpu.SMEM)
    sums = [(HEAD_SIZE, rows), (8, rows)]
    out_shape = [(blocks, HEAD_SIZE + 8, each)] if last else sums
    slots, width = cells.shape[:2]
    tall = ROW_BLOCKS * each
    keys = slots * width
    return pl.pallas_call(
        functools.partial(attend_kernel, len(pieces), fresh is not None, state is not None, last),
        out_shape=[jax.ShapeDtypeStruct(shape, jnp.float32) for shape in out_shape],
        in_specs=in_specs,
        out_specs=[pl.BlockSpec(memory_space=pltpu.VMEM)] * len(out_shape),
        scratch_shapes=[
            pltpu.SMEM((2, slots * (rows // tall) + 2), jnp.int32),
            pltpu.VMEM((slots, width, HEAD_SIZE), jnp.bfloat16),
            pltpu.VMEM((slots, HEAD_SIZE, width), jnp.bfloat16),
            pltpu.VMEM((width, tall), jnp.float32),
            pltpu.VMEM((width, tall), jnp.float32),
            pltpu.VMEM((8, tall), jnp.float32),
            pltpu.VMEM((8, tall), jnp.float32),
        ]
        + [pltpu.VMEM(shape if last else (8, HEAD_SIZE), jnp.float32) for shape in sums],
        compiler_params=pltpu.CompilerParams(vmem_limit_bytes=VMEM_LIMIT),
        cost_estimate=pl.CostEstimate(
            flops=2 * 2 * rows * keys * HEAD_SIZE,
            bytes_accessed=8 * 1024 * 1024,
            transcendentals=rows * keys,
        ),
        name="attend",
    )(*operands)


def merge_kernel(parts_ref, out_ref):
    local = out_ref.shape[0]
    for h in range(parts_ref.shape[0] // HALVES):
        both = [parts_ref[h * HALVES + b] for b in range(HALVES)]
        peaks = [part[HEAD_SIZE : HEAD_SIZE + 1] for part in both]
        masses = [part[HEAD_SIZE + 1 : HEAD_SIZE + 2] for part in both]
        top = jnp.maximum(peaks[0], peaks[1])
        factors = [jnp.exp2((peak - top) * LOG2_SCALE) for peak in peaks]
        whole = factors[0] * masses[0] + factors[1] * masses[1]
        mixed = sum(
            part[:HEAD_SIZE] * (factor / whole) for part, factor in zip(both, factors)
        ).T.astype(out_ref.dtype)
        for g in range(GROUP):
            place = (h * GROUP + g) * HEAD_SIZE
            out_ref[:, place : place + HEAD_SIZE] = mixed[g * local : (g + 1) * local]


def merge(parts, local):
    heads = parts.shape[0] // HALVES
    return pl.pallas_call(
        merge_kernel,
        out_shape=jax.ShapeDtypeStruct((local, heads * GROUP * HEAD_SIZE), jnp.bfloat16),
        in_specs=[pl.BlockSpec(memory_space=pltpu.VMEM)],
        out_specs=pl.BlockSpec(memory_space=pltpu.VMEM),
        compiler_params=pltpu.CompilerParams(vmem_limit_bytes=VMEM_LIMIT),
        name="merge",
    )(parts)


def spread(column):
    return jnp.broadcast_to(column, column.shape[:-1] + (HEAD_SIZE,))


def shards(queries, fresh_kv, pool_key_values, holder_map, passage_lists, recompute):
    requests = lax.axis_size("req")
    members = lax.axis_size("ctx")
    me, member = lax.axis_index("req"), lax.axis_index("ctx")
    half = member % HALVES
    length = pool_key_values.shape[1]
    local = queries.shape[1]
    count = passage_lists.shape[1]
    span = length // (requests * HALVES)
    positions = recompute[0]

    with jax.named_scope("send_queries"):
        parts = address(queries[0], fresh_kv[0])
        parts = lax.all_to_all(parts, "ctx", split_axis=0, concat_axis=0, tiled=True)
    pieces = cut(pool_key_values[0], requests)
    parts, pieces = lax.optimization_barrier((parts, pieces))
    with jax.named_scope("scatter_pool"):
        pieces = lax.all_to_all(pieces, ("req", "ctx"), split_axis=0, concat_axis=0, tiled=True)
    own_queries, fresh = collect(parts, local)

    turn = jnp.arange(requests, dtype=jnp.int32) ^ me
    offsets = jnp.arange(span, dtype=jnp.int32)
    cells = (
        jnp.arange(count, dtype=jnp.int32)[None, :, None] * length
        + turn[:, None, None] * (length // requests)
        + half * span
        + offsets[None, None, :]
    )
    redone = jnp.any(cells[..., None] == positions, axis=-1)
    cells = jnp.where(redone, NEVER, cells).reshape(requests, count // CHUNK, CHUNK * span, 1)
    fresh_cells = positions.reshape(members, HALVES, local // HALVES) - 1
    fresh_cells = lax.dynamic_index_in_dim(fresh_cells, half, 1, keepdims=False)
    fresh_cells = fresh_cells.reshape(-1, len(TURNS[0]) * CHUNK * span, 1)
    row_pos = jnp.broadcast_to(positions.reshape(members, 1, local), (members, GROUP, local))
    row_pos = row_pos.reshape(1, -1)
    reach = CHUNK * length
    steps = (positions.reshape(members, local)[:, -1] + (reach - 1)) // reach

    wanted = holder_map[passage_lists][turn]
    nothing = jnp.full((1,) + fresh_cells.shape[1:], NEVER, jnp.int32)
    place = spread(jnp.concatenate([fresh_cells, nothing]))
    state = attend(steps, own_queries, row_pos, place, [], fresh)
    *state, pieces = lax.optimization_barrier((*state, pieces))
    picked = pick(wanted, pieces)
    with jax.named_scope("send_pieces"):
        arrived = {0: picked[0]}
        for d in (2, 3, 6, 7, 1):
            arrived[d] = swap(picked[d], "req", d)

    for n, group in enumerate(TURNS):
        place = [jnp.concatenate([cells[d] for d in group], axis=1), nothing]
        state = attend(
            steps,
            own_queries,
            row_pos,
            spread(jnp.concatenate(place)),
            [arrived[d] for d in group],
            None,
            state,
            n == len(TURNS) - 1,
        )
        if n == 0:
            *state, far, farther = lax.optimization_barrier((*state, picked[4], picked[5]))
            with jax.named_scope("send_pieces"):
                arrived[4], arrived[5] = swap(far, "req", 4), swap(farther, "req", 5)
    with jax.named_scope("send_sums"):
        parts = lax.all_to_all(state[0], "ctx", split_axis=0, concat_axis=0, tiled=True)
    return merge(parts, local)[None]


def solution(mesh):
    in_specs = (
        P("req", "ctx", None),
        P("req", "ctx", None),
        P(("req", "ctx"), None, None),
        P(),
        P(),
        P("req", None),
    )
    out_specs = P("req", "ctx", None)
    return jax.shard_map(shards, mesh=mesh, in_specs=in_specs, out_specs=out_specs, check_vma=False)
```

```python
import functools

import jax
import jax.numpy as jnp
from jax import lax
from jax.experimental import pallas as pl
from jax.experimental.pallas import tpu as pltpu
from jax.sharding import PartitionSpec as P

KEY_VALUE_HEADS = 8
HEAD_SIZE = 128
GROUP = 4
HALVES = 2

MASKED_SCORE = -3e30
FIRST_PEAK = -1e30
NEVER = 1 << 30
LOG2_SCALE = 1.4426950408889634 / HEAD_SIZE**0.5
ROW_BLOCKS = 2
CHUNK = 4
TURNS = ((0, 1), (2, 3), (6, 7), (4, 5))
VMEM_LIMIT = 16 * 1024 * 1024


def cut_kernel(block_ref, out_ref, sem):
    for h in range(KEY_VALUE_HEADS):
        for which in range(2):
            column = (which * KEY_VALUE_HEADS + h) * HEAD_SIZE
            for b in range(HALVES):
                pltpu.make_async_copy(
                    block_ref.at[:, b, :, column : column + HEAD_SIZE],
                    out_ref.at[:, h, b, which],
                    sem,
                ).start()
    pltpu.make_async_copy(out_ref, out_ref, sem).wait()


def cut(block, requests):
    length, wide = block.shape
    span = length // (requests * HALVES)
    pieces = pl.pallas_call(
        cut_kernel,
        out_shape=jax.ShapeDtypeStruct(
            (requests, KEY_VALUE_HEADS, HALVES, 2, span, HEAD_SIZE), block.dtype
        ),
        in_specs=[pl.BlockSpec(memory_space=pl.ANY)],
        out_specs=pl.BlockSpec(memory_space=pl.ANY),
        scratch_shapes=[pltpu.SemaphoreType.DMA],
        compiler_params=pltpu.CompilerParams(vmem_limit_bytes=VMEM_LIMIT),
        name="cut",
    )(block.reshape(requests, HALVES, span, wide))
    return pieces.reshape(-1, 2, span, HEAD_SIZE)


def address_kernel(queries_ref, fresh_ref, out_ref):
    local = queries_ref.shape[0]
    part = local // HALVES
    rows = GROUP * local
    for h in range(KEY_VALUE_HEADS):
        for g in range(GROUP):
            column = (h * GROUP + g) * HEAD_SIZE
            tile = queries_ref[:, column : column + HEAD_SIZE]
            for b in range(HALVES):
                out_ref[h * HALVES + b, g * local : (g + 1) * local, :] = tile
        for which in range(2):
            column = (which * KEY_VALUE_HEADS + h) * HEAD_SIZE
            for b in range(HALVES):
                out_ref[h * HALVES + b, rows + which * part : rows + (which + 1) * part, :] = (
                    fresh_ref[b * part : (b + 1) * part, column : column + HEAD_SIZE]
                )


def address(queries, fresh):
    local = queries.shape[0]
    shape = (KEY_VALUE_HEADS * HALVES, (GROUP + 1) * local, HEAD_SIZE)
    return pl.pallas_call(
        address_kernel,
        out_shape=jax.ShapeDtypeStruct(shape, queries.dtype),
        in_specs=[pl.BlockSpec(memory_space=pltpu.VMEM)] * 2,
        out_specs=pl.BlockSpec(memory_space=pltpu.VMEM),
        name="address",
    )(queries, fresh)


def collect_kernel(parts_ref, queries_ref, fresh_ref):
    rows = parts_ref.shape[1] - fresh_ref.shape[1]
    for c in range(parts_ref.shape[0]):
        queries_ref[:, c * rows : (c + 1) * rows] = parts_ref[c, :rows, :].T
        fresh_ref[c] = parts_ref[c, rows:, :]


def collect(parts, local):
    count, tall = parts.shape[:2]
    rows = GROUP * local
    return pl.pallas_call(
        collect_kernel,
        out_shape=[
            jax.ShapeDtypeStruct((HEAD_SIZE, count * rows), parts.dtype),
            jax.ShapeDtypeStruct((count, tall - rows, HEAD_SIZE), parts.dtype),
        ],
        in_specs=[pl.BlockSpec(memory_space=pltpu.VMEM)],
        out_specs=[pl.BlockSpec(memory_space=pltpu.VMEM)] * 2,
        name="collect",
    )(parts)


def swap(pieces, axis, far):
    return lax.ppermute(pieces, axis, [(i, i ^ far) for i in range(lax.axis_size(axis))])


def pick_kernel(wanted_ref, pieces_ref, *rest):
    outs, sems = rest[:-1], rest[-1]
    count = outs[0].shape[0]
    for d, out in enumerate(outs):
        for j in range(count):
            slot = wanted_ref[d, j]
            pltpu.make_async_copy(pieces_ref.at[slot], out.at[j], sems.at[d]).start()
    for d, out in enumerate(outs):
        pltpu.make_async_copy(out, out, sems.at[d]).wait()


def pick(wanted, pieces):
    turns, count = wanted.shape
    shape = jax.ShapeDtypeStruct((count,) + pieces.shape[1:], pieces.dtype)
    return pl.pallas_call(
        pick_kernel,
        out_shape=[shape] * turns,
        in_specs=[
            pl.BlockSpec(memory_space=pltpu.SMEM),
            pl.BlockSpec(memory_space=pltpu.VMEM),
        ],
        out_specs=[pl.BlockSpec(memory_space=pl.ANY)] * turns,
        scratch_shapes=[pltpu.SemaphoreType.DMA((turns,))],
        compiler_params=pltpu.CompilerParams(vmem_limit_bytes=VMEM_LIMIT),
        cost_estimate=pl.CostEstimate(flops=0, bytes_accessed=2 * pieces.size * 2, transcendentals=0),
        name="pick",
    )(wanted, pieces)


def attend_kernel(piece_count, with_fresh, with_state, last, *refs):
    refs = list(refs)
    pairs_ref, keys_ref, values_ref, *buffers = refs[-9:]
    refs = refs[:-9]
    scores, peaks = buffers[0:2], buffers[2:4]
    if last:
        sum_ref, stats_ref = buffers[4:6]
    steps_ref = refs.pop(0)
    queries_ref = refs.pop(0)
    row_ref = refs.pop(0)
    cell_ref = refs.pop(0)
    pieces = [refs.pop(0) for _ in range(piece_count)]
    if with_fresh:
        fresh_ref = refs.pop(0)
    if with_state:
        sum_in, stats_in = refs.pop(0), refs.pop(0)
    if last:
        (out,) = refs
    else:
        sum_ref, stats_ref = refs
    blocks = steps_ref.shape[0]
    each = queries_ref.shape[1] // blocks
    rows = ROW_BLOCKS * each
    width = keys_ref.shape[1]
    repeats = rows // HEAD_SIZE
    cached_slots = pieces[0].shape[0] // CHUNK if pieces else 0
    nothing = cell_ref.shape[0] - 1

    if pieces:

        @pl.loop(0, steps_ref[blocks - 1])
        def _(s):
            parts = [piece[pl.ds(s * CHUNK, CHUNK)] for piece in pieces]
            for which, ref in ((0, keys_ref), (1, values_ref)):
                lines = [part[:, which].reshape(-1, HEAD_SIZE) for part in parts]
                lines = jnp.concatenate(lines, axis=0)
                ref[s] = lines.T if which else lines

    keys_ref[nothing] = jnp.zeros(keys_ref.shape[1:], keys_ref.dtype)
    values_ref[nothing] = jnp.zeros(values_ref.shape[1:], values_ref.dtype)
    if with_fresh:
        half = fresh_ref.shape[1] // 2
        per = width // half
        for f in range(blocks // per):
            part = fresh_ref[f * per : (f + 1) * per]
            keys_ref[cached_slots + f] = part[:, :half].reshape(width, HEAD_SIZE)
            values_ref[cached_slots + f] = part[:, half:].reshape(width, HEAD_SIZE).T
    if with_state:
        sum_ref[...] = sum_in[...]
        stats_ref[...] = stats_in[...]
    else:
        sum_ref[...] = jnp.zeros(sum_ref.shape, jnp.float32)
        line = lax.broadcasted_iota(jnp.int32, stats_ref.shape, 0)
        stats_ref[...] = jnp.where(line == 0, FIRST_PEAK, 0.0)

    total = jnp.int32(0)
    for block in range(blocks // ROW_BLOCKS):
        final = (block + 1) * ROW_BLOCKS - 1

        def add(s, total, block=block):
            pairs_ref[0, total] = block
            pairs_ref[1, total] = s
            return total + 1

        if pieces:
            total = lax.fori_loop(0, steps_ref[final], add, total)
        if with_fresh:
            total = lax.fori_loop(cached_slots, cached_slots + final // per + 1, add, total)
    for n in range(2):
        pairs_ref[0, total + n] = 0
        pairs_ref[1, total + n] = nothing

    def place(block):
        return pl.ds(pl.multiple_of(block * rows, rows), rows)

    def score(t, side):
        mine, slot = place(pairs_ref[0, t]), pairs_ref[1, t]
        raw = jnp.dot(keys_ref[slot], queries_ref[:, mine], preferred_element_type=jnp.float32)
        usable = jnp.concatenate([cell_ref[slot]] * repeats, axis=1) < row_ref[:, mine]
        masked = jnp.where(usable, raw, MASKED_SCORE)
        scores[side][...] = masked
        peaks[side][...] = jnp.max(masked.reshape(width // 8, 8, rows), axis=0)

    def weigh(t, side):
        mine, slot = place(pairs_ref[0, t]), pairs_ref[1, t]
        old = stats_ref[0:1, mine]
        peak = jnp.maximum(old, jnp.max(peaks[side][...], axis=0, keepdims=True))
        weights = jnp.exp2((scores[side][...] - peak) * LOG2_SCALE)
        keep = jnp.exp2((old - peak) * LOG2_SCALE)
        mass = jnp.sum(weights.reshape(width // 8, 8, rows), axis=0)
        stats_ref[0:1, mine] = peak
        stats_ref[1:2, mine] = stats_ref[1:2, mine] * keep + jnp.sum(mass, axis=0, keepdims=True)
        sum_ref[:, mine] = sum_ref[:, mine] * keep + jnp.dot(
            values_ref[slot], weights.astype(jnp.bfloat16), preferred_element_type=jnp.float32
        )

    score(0, 0)

    @pl.loop(0, (total + 1) // 2)
    def _(u):
        score(2 * u + 1, 1)
        weigh(2 * u, 0)
        score(2 * u + 2, 0)
        weigh(2 * u + 1, 1)

    if last:
        for b in range(blocks):
            part = slice(b * each, (b + 1) * each)
            out[b, :HEAD_SIZE, :] = sum_ref[:, part]
            out[b, HEAD_SIZE:, :] = stats_ref[:, part]


def attend(steps, queries, row_pos, cells, pieces, fresh=None, state=None, last=False):
    blocks, rows = steps.shape[0], queries.shape[1]
    each = rows // blocks
    operands = [steps, queries, row_pos, cells, *pieces]
    if fresh is not None:
        operands.append(fresh)
    if state is not None:
        operands += list(state)
    in_specs = [pl.BlockSpec(memory_space=pltpu.VMEM)] * len(operands)
    in_specs[0] = pl.BlockSpec(memory_space=pltpu.SMEM)
    sums = [(HEAD_SIZE, rows), (8, rows)]
    out_shape = [(blocks, HEAD_SIZE + 8, each)] if last else sums
    slots, width = cells.shape[:2]
    tall = ROW_BLOCKS * each
    keys = slots * width
    return pl.pallas_call(
        functools.partial(attend_kernel, len(pieces), fresh is not None, state is not None, last),
        out_shape=[jax.ShapeDtypeStruct(shape, jnp.float32) for shape in out_shape],
        in_specs=in_specs,
        out_specs=[pl.BlockSpec(memory_space=pltpu.VMEM)] * len(out_shape),
        scratch_shapes=[
            pltpu.SMEM((2, slots * (rows // tall) + 2), jnp.int32),
            pltpu.VMEM((slots, width, HEAD_SIZE), jnp.bfloat16),
            pltpu.VMEM((slots, HEAD_SIZE, width), jnp.bfloat16),
            pltpu.VMEM((width, tall), jnp.float32),
            pltpu.VMEM((width, tall), jnp.float32),
            pltpu.VMEM((8, tall), jnp.float32),
            pltpu.VMEM((8, tall), jnp.float32),
        ]
        + [pltpu.VMEM(shape if last else (8, HEAD_SIZE), jnp.float32) for shape in sums],
        compiler_params=pltpu.CompilerParams(vmem_limit_bytes=VMEM_LIMIT),
        cost_estimate=pl.CostEstimate(
            flops=2 * 2 * rows * keys * HEAD_SIZE,
            bytes_accessed=8 * 1024 * 1024,
            transcendentals=rows * keys,
        ),
        name="attend",
    )(*operands)


def merge_kernel(parts_ref, out_ref):
    local = out_ref.shape[0]
    for h in range(parts_ref.shape[0] // HALVES):
        both = [parts_ref[h * HALVES + b] for b in range(HALVES)]
        peaks = [part[HEAD_SIZE : HEAD_SIZE + 1] for part in both]
        masses = [part[HEAD_SIZE + 1 : HEAD_SIZE + 2] for part in both]
        top = jnp.maximum(peaks[0], peaks[1])
        factors = [jnp.exp2((peak - top) * LOG2_SCALE) for peak in peaks]
        whole = factors[0] * masses[0] + factors[1] * masses[1]
        mixed = sum(
            part[:HEAD_SIZE] * (factor / whole) for part, factor in zip(both, factors)
        ).T.astype(out_ref.dtype)
        for g in range(GROUP):
            place = (h * GROUP + g) * HEAD_SIZE
            out_ref[:, place : place + HEAD_SIZE] = mixed[g * local : (g + 1) * local]


def merge(parts, local):
    heads = parts.shape[0] // HALVES
    return pl.pallas_call(
        merge_kernel,
        out_shape=jax.ShapeDtypeStruct((local, heads * GROUP * HEAD_SIZE), jnp.bfloat16),
        in_specs=[pl.BlockSpec(memory_space=pltpu.VMEM)],
        out_specs=pl.BlockSpec(memory_space=pltpu.VMEM),
        compiler_params=pltpu.CompilerParams(vmem_limit_bytes=VMEM_LIMIT),
        name="merge",
    )(parts)


def spread(column):
    return jnp.broadcast_to(column, column.shape[:-1] + (HEAD_SIZE,))


def shards(queries, fresh_kv, pool_key_values, holder_map, passage_lists, recompute):
    requests = lax.axis_size("req")
    members = lax.axis_size("ctx")
    me, member = lax.axis_index("req"), lax.axis_index("ctx")
    half = member % HALVES
    length = pool_key_values.shape[1]
    local = queries.shape[1]
    count = passage_lists.shape[1]
    span = length // (requests * HALVES)
    positions = recompute[0]

    pieces = cut(pool_key_values[0], requests)
    with jax.named_scope("scatter_pool"):
        pieces = lax.all_to_all(pieces, ("req", "ctx"), split_axis=0, concat_axis=0, tiled=True)
    with jax.named_scope("send_queries"):
        parts = address(queries[0], fresh_kv[0])
        parts = lax.all_to_all(parts, "ctx", split_axis=0, concat_axis=0, tiled=True)
    own_queries, fresh = collect(parts, local)

    turn = jnp.arange(requests, dtype=jnp.int32) ^ me
    offsets = jnp.arange(span, dtype=jnp.int32)
    cells = (
        jnp.arange(count, dtype=jnp.int32)[None, :, None] * length
        + turn[:, None, None] * (length // requests)
        + half * span
        + offsets[None, None, :]
    )
    redone = jnp.any(cells[..., None] == positions, axis=-1)
    cells = jnp.where(redone, NEVER, cells).reshape(requests, count // CHUNK, CHUNK * span, 1)
    fresh_cells = positions.reshape(members, HALVES, local // HALVES) - 1
    fresh_cells = lax.dynamic_index_in_dim(fresh_cells, half, 1, keepdims=False)
    fresh_cells = fresh_cells.reshape(-1, len(TURNS[0]) * CHUNK * span, 1)
    row_pos = jnp.broadcast_to(positions.reshape(members, 1, local), (members, GROUP, local))
    row_pos = row_pos.reshape(1, -1)
    reach = CHUNK * length
    steps = (positions.reshape(members, local)[:, -1] + (reach - 1)) // reach

    wanted = holder_map[passage_lists][turn]
    picked = pick(wanted, pieces)
    with jax.named_scope("send_pieces"):
        arrived = {0: picked[0]}
        for d in (2, 3, 6, 7, 1):
            arrived[d] = swap(picked[d], "req", d)

    nothing = jnp.full((1,) + fresh_cells.shape[1:], NEVER, jnp.int32)
    place = spread(jnp.concatenate([fresh_cells, nothing]))
    state = attend(steps, own_queries, row_pos, place, [], fresh)
    *state, arrived[2], arrived[3], far, farther = lax.optimization_barrier(
        (*state, arrived[2], arrived[3], picked[4], picked[5])
    )
    with jax.named_scope("send_pieces"):
        arrived[4], arrived[5] = swap(far, "req", 4), swap(farther, "req", 5)
    for n, group in enumerate(TURNS):
        place = [jnp.concatenate([cells[d] for d in group], axis=1), nothing]
        state = attend(
            steps,
            own_queries,
            row_pos,
            spread(jnp.concatenate(place)),
            [arrived[d] for d in group],
            None,
            state,
            n == len(TURNS) - 1,
        )
    with jax.named_scope("send_sums"):
        parts = lax.all_to_all(state[0], "ctx", split_axis=0, concat_axis=0, tiled=True)
    return merge(parts, local)[None]


def solution(mesh):
    in_specs = (
        P("req", "ctx", None),
        P("req", "ctx", None),
        P(("req", "ctx"), None, None),
        P(),
        P(),
        P("req", None),
    )
    out_specs = P("req", "ctx", None)
    return jax.shard_map(shards, mesh=mesh, in_specs=in_specs, out_specs=out_specs, check_vma=False)
```

```python
import functools

import jax
import jax.numpy as jnp
from jax import lax
from jax.experimental import pallas as pl
from jax.experimental.pallas import tpu as pltpu
from jax.sharding import PartitionSpec as P

KEY_VALUE_HEADS = 8
HEAD_SIZE = 128
GROUP = 4
HALVES = 2

MASKED_SCORE = -3e30
FIRST_PEAK = -1e30
NEVER = 1 << 30
LOG2_SCALE = 1.4426950408889634 / HEAD_SIZE**0.5
ROW_BLOCKS = 2
CHUNK = 4
TURNS = ((0, 1), (2, 3), (6, 7), (4, 5))
VMEM_LIMIT = 16 * 1024 * 1024


def cut_kernel(block_ref, out_ref, sem):
    for h in range(KEY_VALUE_HEADS):
        for which in range(2):
            column = (which * KEY_VALUE_HEADS + h) * HEAD_SIZE
            for b in range(HALVES):
                pltpu.make_async_copy(
                    block_ref.at[:, b, :, column : column + HEAD_SIZE],
                    out_ref.at[:, h, b, which],
                    sem,
                ).start()
    pltpu.make_async_copy(out_ref, out_ref, sem).wait()


def cut(block, requests):
    length, wide = block.shape
    span = length // (requests * HALVES)
    pieces = pl.pallas_call(
        cut_kernel,
        out_shape=jax.ShapeDtypeStruct(
            (requests, KEY_VALUE_HEADS, HALVES, 2, span, HEAD_SIZE), block.dtype
        ),
        in_specs=[pl.BlockSpec(memory_space=pl.ANY)],
        out_specs=pl.BlockSpec(memory_space=pl.ANY),
        scratch_shapes=[pltpu.SemaphoreType.DMA],
        compiler_params=pltpu.CompilerParams(vmem_limit_bytes=VMEM_LIMIT),
        name="cut",
    )(block.reshape(requests, HALVES, span, wide))
    return pieces.reshape(-1, 2, span, HEAD_SIZE)


def address_kernel(queries_ref, fresh_ref, out_ref):
    local = queries_ref.shape[0]
    part = local // HALVES
    rows = GROUP * local
    for h in range(KEY_VALUE_HEADS):
        for g in range(GROUP):
            column = (h * GROUP + g) * HEAD_SIZE
            tile = queries_ref[:, column : column + HEAD_SIZE]
            for b in range(HALVES):
                out_ref[h * HALVES + b, g * local : (g + 1) * local, :] = tile
        for which in range(2):
            column = (which * KEY_VALUE_HEADS + h) * HEAD_SIZE
            for b in range(HALVES):
                out_ref[h * HALVES + b, rows + which * part : rows + (which + 1) * part, :] = (
                    fresh_ref[b * part : (b + 1) * part, column : column + HEAD_SIZE]
                )


def address(queries, fresh):
    local = queries.shape[0]
    shape = (KEY_VALUE_HEADS * HALVES, (GROUP + 1) * local, HEAD_SIZE)
    return pl.pallas_call(
        address_kernel,
        out_shape=jax.ShapeDtypeStruct(shape, queries.dtype),
        in_specs=[pl.BlockSpec(memory_space=pltpu.VMEM)] * 2,
        out_specs=pl.BlockSpec(memory_space=pltpu.VMEM),
        name="address",
    )(queries, fresh)


def collect_kernel(parts_ref, queries_ref, fresh_ref):
    rows = parts_ref.shape[1] - fresh_ref.shape[1]
    for c in range(parts_ref.shape[0]):
        queries_ref[:, c * rows : (c + 1) * rows] = parts_ref[c, :rows, :].T
        fresh_ref[c] = parts_ref[c, rows:, :]


def collect(parts, local):
    count, tall = parts.shape[:2]
    rows = GROUP * local
    return pl.pallas_call(
        collect_kernel,
        out_shape=[
            jax.ShapeDtypeStruct((HEAD_SIZE, count * rows), parts.dtype),
            jax.ShapeDtypeStruct((count, tall - rows, HEAD_SIZE), parts.dtype),
        ],
        in_specs=[pl.BlockSpec(memory_space=pltpu.VMEM)],
        out_specs=[pl.BlockSpec(memory_space=pltpu.VMEM)] * 2,
        name="collect",
    )(parts)


def swap(pieces, axis, far):
    return lax.ppermute(pieces, axis, [(i, i ^ far) for i in range(lax.axis_size(axis))])


def pick_kernel(wanted_ref, pieces_ref, *rest):
    outs, sems = rest[:-1], rest[-1]
    count = outs[0].shape[0]
    for d, out in enumerate(outs):
        for j in range(count):
            slot = wanted_ref[d, j]
            pltpu.make_async_copy(pieces_ref.at[slot], out.at[j], sems.at[d]).start()
    for d, out in enumerate(outs):
        pltpu.make_async_copy(out, out, sems.at[d]).wait()


def pick(wanted, pieces):
    turns, count = wanted.shape
    shape = jax.ShapeDtypeStruct((count,) + pieces.shape[1:], pieces.dtype)
    return pl.pallas_call(
        pick_kernel,
        out_shape=[shape] * turns,
        in_specs=[
            pl.BlockSpec(memory_space=pltpu.SMEM),
            pl.BlockSpec(memory_space=pltpu.VMEM),
        ],
        out_specs=[pl.BlockSpec(memory_space=pl.ANY)] * turns,
        scratch_shapes=[pltpu.SemaphoreType.DMA((turns,))],
        compiler_params=pltpu.CompilerParams(vmem_limit_bytes=VMEM_LIMIT),
        cost_estimate=pl.CostEstimate(flops=0, bytes_accessed=2 * pieces.size * 2, transcendentals=0),
        name="pick",
    )(wanted, pieces)


def attend_kernel(piece_count, with_fresh, with_state, last, *refs):
    refs = list(refs)
    pairs_ref, keys_ref, values_ref, *buffers = refs[-9:]
    refs = refs[:-9]
    scores, peaks = buffers[0:2], buffers[2:4]
    if last:
        sum_ref, stats_ref = buffers[4:6]
    steps_ref = refs.pop(0)
    queries_ref = refs.pop(0)
    row_ref = refs.pop(0)
    cell_ref = refs.pop(0)
    pieces = [refs.pop(0) for _ in range(piece_count)]
    if with_fresh:
        fresh_ref = refs.pop(0)
    if with_state:
        sum_in, stats_in = refs.pop(0), refs.pop(0)
    if last:
        (out,) = refs
    else:
        sum_ref, stats_ref = refs
    blocks = steps_ref.shape[0]
    each = queries_ref.shape[1] // blocks
    rows = ROW_BLOCKS * each
    width = keys_ref.shape[1]
    repeats = rows // HEAD_SIZE
    cached_slots = pieces[0].shape[0] // CHUNK
    nothing = cell_ref.shape[0] - 1

    @pl.loop(0, steps_ref[blocks - 1])
    def _(s):
        parts = [piece[pl.ds(s * CHUNK, CHUNK)] for piece in pieces]
        keys_ref[s] = jnp.concatenate([p[:, 0].reshape(-1, HEAD_SIZE) for p in parts], axis=0)
        values_ref[s] = jnp.concatenate([p[:, 1].reshape(-1, HEAD_SIZE) for p in parts], axis=0).T

    keys_ref[nothing] = jnp.zeros(keys_ref.shape[1:], keys_ref.dtype)
    values_ref[nothing] = jnp.zeros(values_ref.shape[1:], values_ref.dtype)
    if with_fresh:
        half = fresh_ref.shape[1] // 2
        per = width // half
        for f in range(blocks // per):
            part = fresh_ref[f * per : (f + 1) * per]
            keys_ref[cached_slots + f] = part[:, :half].reshape(width, HEAD_SIZE)
            values_ref[cached_slots + f] = part[:, half:].reshape(width, HEAD_SIZE).T
    if with_state:
        sum_ref[...] = sum_in[...]
        stats_ref[...] = stats_in[...]
    else:
        sum_ref[...] = jnp.zeros(sum_ref.shape, jnp.float32)
        line = lax.broadcasted_iota(jnp.int32, stats_ref.shape, 0)
        stats_ref[...] = jnp.where(line == 0, FIRST_PEAK, 0.0)

    total = jnp.int32(0)
    for block in range(blocks // ROW_BLOCKS):
        final = (block + 1) * ROW_BLOCKS - 1

        def add(s, total, block=block):
            pairs_ref[0, total] = block
            pairs_ref[1, total] = s
            return total + 1

        total = lax.fori_loop(0, steps_ref[final], add, total)
        if with_fresh:
            total = lax.fori_loop(cached_slots, cached_slots + final // per + 1, add, total)
    for n in range(2):
        pairs_ref[0, total + n] = 0
        pairs_ref[1, total + n] = nothing

    def place(block):
        return pl.ds(pl.multiple_of(block * rows, rows), rows)

    def score(t, side):
        mine, slot = place(pairs_ref[0, t]), pairs_ref[1, t]
        raw = jnp.dot(keys_ref[slot], queries_ref[:, mine], preferred_element_type=jnp.float32)
        usable = jnp.concatenate([cell_ref[slot]] * repeats, axis=1) < row_ref[:, mine]
        masked = jnp.where(usable, raw, MASKED_SCORE)
        scores[side][...] = masked
        peaks[side][...] = jnp.max(masked.reshape(width // 8, 8, rows), axis=0)

    def weigh(t, side):
        mine, slot = place(pairs_ref[0, t]), pairs_ref[1, t]
        old = stats_ref[0:1, mine]
        peak = jnp.maximum(old, jnp.max(peaks[side][...], axis=0, keepdims=True))
        weights = jnp.exp2((scores[side][...] - peak) * LOG2_SCALE)
        keep = jnp.exp2((old - peak) * LOG2_SCALE)
        mass = jnp.sum(weights.reshape(width // 8, 8, rows), axis=0)
        stats_ref[0:1, mine] = peak
        stats_ref[1:2, mine] = stats_ref[1:2, mine] * keep + jnp.sum(mass, axis=0, keepdims=True)
        sum_ref[:, mine] = sum_ref[:, mine] * keep + jnp.dot(
            values_ref[slot], weights.astype(jnp.bfloat16), preferred_element_type=jnp.float32
        )

    score(0, 0)

    @pl.loop(0, (total + 1) // 2)
    def _(u):
        score(2 * u + 1, 1)
        weigh(2 * u, 0)
        score(2 * u + 2, 0)
        weigh(2 * u + 1, 1)

    if last:
        for b in range(blocks):
            part = slice(b * each, (b + 1) * each)
            out[b, :HEAD_SIZE, :] = sum_ref[:, part]
            out[b, HEAD_SIZE:, :] = stats_ref[:, part]


def attend(steps, queries, row_pos, cells, pieces, fresh=None, state=None, last=False):
    blocks, rows = steps.shape[0], queries.shape[1]
    each = rows // blocks
    operands = [steps, queries, row_pos, cells, *pieces]
    if fresh is not None:
        operands.append(fresh)
    if state is not None:
        operands += list(state)
    in_specs = [pl.BlockSpec(memory_space=pltpu.VMEM)] * len(operands)
    in_specs[0] = pl.BlockSpec(memory_space=pltpu.SMEM)
    sums = [(HEAD_SIZE, rows), (8, rows)]
    out_shape = [(blocks, HEAD_SIZE + 8, each)] if last else sums
    slots, width = cells.shape[:2]
    tall = ROW_BLOCKS * each
    keys = slots * width
    return pl.pallas_call(
        functools.partial(attend_kernel, len(pieces), fresh is not None, state is not None, last),
        out_shape=[jax.ShapeDtypeStruct(shape, jnp.float32) for shape in out_shape],
        in_specs=in_specs,
        out_specs=[pl.BlockSpec(memory_space=pltpu.VMEM)] * len(out_shape),
        scratch_shapes=[
            pltpu.SMEM((2, slots * (rows // tall) + 2), jnp.int32),
            pltpu.VMEM((slots, width, HEAD_SIZE), jnp.bfloat16),
            pltpu.VMEM((slots, HEAD_SIZE, width), jnp.bfloat16),
            pltpu.VMEM((width, tall), jnp.float32),
            pltpu.VMEM((width, tall), jnp.float32),
            pltpu.VMEM((8, tall), jnp.float32),
            pltpu.VMEM((8, tall), jnp.float32),
        ]
        + [pltpu.VMEM(shape if last else (8, HEAD_SIZE), jnp.float32) for shape in sums],
        compiler_params=pltpu.CompilerParams(vmem_limit_bytes=VMEM_LIMIT),
        cost_estimate=pl.CostEstimate(
            flops=2 * 2 * rows * keys * HEAD_SIZE,
            bytes_accessed=8 * 1024 * 1024,
            transcendentals=rows * keys,
        ),
        name="attend",
    )(*operands)


def merge_kernel(parts_ref, out_ref):
    local = out_ref.shape[0]
    for h in range(parts_ref.shape[0] // HALVES):
        both = [parts_ref[h * HALVES + b] for b in range(HALVES)]
        peaks = [part[HEAD_SIZE : HEAD_SIZE + 1] for part in both]
        masses = [part[HEAD_SIZE + 1 : HEAD_SIZE + 2] for part in both]
        top = jnp.maximum(peaks[0], peaks[1])
        factors = [jnp.exp2((peak - top) * LOG2_SCALE) for peak in peaks]
        whole = factors[0] * masses[0] + factors[1] * masses[1]
        mixed = sum(
            part[:HEAD_SIZE] * (factor / whole) for part, factor in zip(both, factors)
        ).T.astype(out_ref.dtype)
        for g in range(GROUP):
            place = (h * GROUP + g) * HEAD_SIZE
            out_ref[:, place : place + HEAD_SIZE] = mixed[g * local : (g + 1) * local]


def merge(parts, local):
    heads = parts.shape[0] // HALVES
    return pl.pallas_call(
        merge_kernel,
        out_shape=jax.ShapeDtypeStruct((local, heads * GROUP * HEAD_SIZE), jnp.bfloat16),
        in_specs=[pl.BlockSpec(memory_space=pltpu.VMEM)],
        out_specs=pl.BlockSpec(memory_space=pltpu.VMEM),
        compiler_params=pltpu.CompilerParams(vmem_limit_bytes=VMEM_LIMIT),
        name="merge",
    )(parts)


def spread(column):
    return jnp.broadcast_to(column, column.shape[:-1] + (HEAD_SIZE,))


def shards(queries, fresh_kv, pool_key_values, holder_map, passage_lists, recompute):
    requests = lax.axis_size("req")
    members = lax.axis_size("ctx")
    me, member = lax.axis_index("req"), lax.axis_index("ctx")
    half = member % HALVES
    length = pool_key_values.shape[1]
    local = queries.shape[1]
    count = passage_lists.shape[1]
    span = length // (requests * HALVES)
    positions = recompute[0]

    pieces = cut(pool_key_values[0], requests)
    with jax.named_scope("scatter_pool"):
        pieces = lax.all_to_all(pieces, ("req", "ctx"), split_axis=0, concat_axis=0, tiled=True)
    with jax.named_scope("send_queries"):
        parts = address(queries[0], fresh_kv[0])
        parts = lax.all_to_all(parts, "ctx", split_axis=0, concat_axis=0, tiled=True)
    own_queries, fresh = collect(parts, local)

    turn = jnp.arange(requests, dtype=jnp.int32) ^ me
    offsets = jnp.arange(span, dtype=jnp.int32)
    cells = (
        jnp.arange(count, dtype=jnp.int32)[None, :, None] * length
        + turn[:, None, None] * (length // requests)
        + half * span
        + offsets[None, None, :]
    )
    redone = jnp.any(cells[..., None] == positions, axis=-1)
    cells = jnp.where(redone, NEVER, cells).reshape(requests, count // CHUNK, CHUNK * span, 1)
    fresh_cells = positions.reshape(members, HALVES, local // HALVES) - 1
    fresh_cells = lax.dynamic_index_in_dim(fresh_cells, half, 1, keepdims=False)
    fresh_cells = fresh_cells.reshape(-1, len(TURNS[0]) * CHUNK * span, 1)
    row_pos = jnp.broadcast_to(positions.reshape(members, 1, local), (members, GROUP, local))
    row_pos = row_pos.reshape(1, -1)
    reach = CHUNK * length
    steps = (positions.reshape(members, local)[:, -1] + (reach - 1)) // reach

    wanted = holder_map[passage_lists][turn]
    picked = pick(wanted, pieces)
    with jax.named_scope("send_pieces"):
        arrived = {0: picked[0]}
        for d in (2, 3, 6, 7, 1):
            arrived[d] = swap(picked[d], "req", d)
        arrived[1], *far = lax.optimization_barrier((arrived[1], picked[4], picked[5]))
        arrived[4], arrived[5] = swap(far[0], "req", 4), swap(far[1], "req", 5)

    nothing = jnp.full((1,) + fresh_cells.shape[1:], NEVER, jnp.int32)
    state = None
    for n, group in enumerate(TURNS):
        place = [jnp.concatenate([cells[d] for d in group], axis=1)]
        if n == 0:
            place.append(fresh_cells)
        place.append(nothing[:, : place[0].shape[1]])
        state = attend(
            steps,
            own_queries,
            row_pos,
            spread(jnp.concatenate(place, axis=0)),
            [arrived[d] for d in group],
            fresh if n == 0 else None,
            state,
            n == len(TURNS) - 1,
        )
    with jax.named_scope("send_sums"):
        parts = lax.all_to_all(state[0], "ctx", split_axis=0, concat_axis=0, tiled=True)
    return merge(parts, local)[None]


def solution(mesh):
    in_specs = (
        P("req", "ctx", None),
        P("req", "ctx", None),
        P(("req", "ctx"), None, None),
        P(),
        P(),
        P("req", None),
    )
    out_specs = P("req", "ctx", None)
    return jax.shard_map(shards, mesh=mesh, in_specs=in_specs, out_specs=out_specs, check_vma=False)
```

```python
import functools

import jax
import jax.numpy as jnp
from jax import lax
from jax.experimental import pallas as pl
from jax.experimental.pallas import tpu as pltpu
from jax.sharding import PartitionSpec as P

KEY_VALUE_HEADS = 8
HEAD_SIZE = 128
GROUP = 4
HALVES = 2

MASKED_SCORE = -3e30
FIRST_PEAK = -1e30
NEVER = 1 << 30
LOG2_SCALE = 1.4426950408889634 / HEAD_SIZE**0.5
ROW_BLOCKS = 2
CHUNK = 4
TURNS = ((0, 1), (2, 3), (6, 7), (4, 5))
VMEM_LIMIT = 16 * 1024 * 1024


def cut_kernel(block_ref, out_ref, sem):
    for h in range(KEY_VALUE_HEADS):
        for which in range(2):
            column = (which * KEY_VALUE_HEADS + h) * HEAD_SIZE
            for b in range(HALVES):
                pltpu.make_async_copy(
                    block_ref.at[:, b, :, column : column + HEAD_SIZE],
                    out_ref.at[:, h, b, which],
                    sem,
                ).start()
    pltpu.make_async_copy(out_ref, out_ref, sem).wait()


def cut(block, requests):
    length, wide = block.shape
    span = length // (requests * HALVES)
    pieces = pl.pallas_call(
        cut_kernel,
        out_shape=jax.ShapeDtypeStruct(
            (requests, KEY_VALUE_HEADS, HALVES, 2, span, HEAD_SIZE), block.dtype
        ),
        in_specs=[pl.BlockSpec(memory_space=pl.ANY)],
        out_specs=pl.BlockSpec(memory_space=pl.ANY),
        scratch_shapes=[pltpu.SemaphoreType.DMA],
        compiler_params=pltpu.CompilerParams(vmem_limit_bytes=VMEM_LIMIT),
        name="cut",
    )(block.reshape(requests, HALVES, span, wide))
    return pieces.reshape(-1, 2, span, HEAD_SIZE)


def address_kernel(queries_ref, fresh_ref, out_ref):
    local = queries_ref.shape[0]
    part = local // HALVES
    rows = GROUP * local
    for h in range(KEY_VALUE_HEADS):
        for g in range(GROUP):
            column = (h * GROUP + g) * HEAD_SIZE
            tile = queries_ref[:, column : column + HEAD_SIZE]
            for b in range(HALVES):
                out_ref[h * HALVES + b, g * local : (g + 1) * local, :] = tile
        for which in range(2):
            column = (which * KEY_VALUE_HEADS + h) * HEAD_SIZE
            for b in range(HALVES):
                out_ref[h * HALVES + b, rows + which * part : rows + (which + 1) * part, :] = (
                    fresh_ref[b * part : (b + 1) * part, column : column + HEAD_SIZE]
                )


def address(queries, fresh):
    local = queries.shape[0]
    shape = (KEY_VALUE_HEADS * HALVES, (GROUP + 1) * local, HEAD_SIZE)
    return pl.pallas_call(
        address_kernel,
        out_shape=jax.ShapeDtypeStruct(shape, queries.dtype),
        in_specs=[pl.BlockSpec(memory_space=pltpu.VMEM)] * 2,
        out_specs=pl.BlockSpec(memory_space=pltpu.VMEM),
        name="address",
    )(queries, fresh)


def collect_kernel(parts_ref, queries_ref, fresh_ref):
    rows = parts_ref.shape[1] - fresh_ref.shape[1]
    for c in range(parts_ref.shape[0]):
        queries_ref[:, c * rows : (c + 1) * rows] = parts_ref[c, :rows, :].T
        fresh_ref[c] = parts_ref[c, rows:, :]


def collect(parts, local):
    count, tall = parts.shape[:2]
    rows = GROUP * local
    return pl.pallas_call(
        collect_kernel,
        out_shape=[
            jax.ShapeDtypeStruct((HEAD_SIZE, count * rows), parts.dtype),
            jax.ShapeDtypeStruct((count, tall - rows, HEAD_SIZE), parts.dtype),
        ],
        in_specs=[pl.BlockSpec(memory_space=pltpu.VMEM)],
        out_specs=[pl.BlockSpec(memory_space=pltpu.VMEM)] * 2,
        name="collect",
    )(parts)


def swap(pieces, axis, far):
    return lax.ppermute(pieces, axis, [(i, i ^ far) for i in range(lax.axis_size(axis))])


def pick_kernel(wanted_ref, pieces_ref, *rest):
    outs, sems = rest[:-1], rest[-1]
    count = outs[0].shape[0]
    for d, out in enumerate(outs):
        for j in range(count):
            slot = wanted_ref[d, j]
            pltpu.make_async_copy(pieces_ref.at[slot], out.at[j], sems.at[d]).start()
    for d, out in enumerate(outs):
        pltpu.make_async_copy(out, out, sems.at[d]).wait()


def pick(wanted, pieces):
    turns, count = wanted.shape
    shape = jax.ShapeDtypeStruct((count,) + pieces.shape[1:], pieces.dtype)
    return pl.pallas_call(
        pick_kernel,
        out_shape=[shape] * turns,
        in_specs=[
            pl.BlockSpec(memory_space=pltpu.SMEM),
            pl.BlockSpec(memory_space=pltpu.VMEM),
        ],
        out_specs=[pl.BlockSpec(memory_space=pl.ANY)] * turns,
        scratch_shapes=[pltpu.SemaphoreType.DMA((turns,))],
        compiler_params=pltpu.CompilerParams(vmem_limit_bytes=VMEM_LIMIT),
        cost_estimate=pl.CostEstimate(flops=0, bytes_accessed=2 * pieces.size * 2, transcendentals=0),
        name="pick",
    )(wanted, pieces)


def attend_kernel(piece_count, with_fresh, with_state, last, *refs):
    refs = list(refs)
    pairs_ref, keys_ref, values_ref, *buffers = refs[-9:]
    refs = refs[:-9]
    scores, peaks = buffers[0:2], buffers[2:4]
    if last:
        sum_ref, stats_ref = buffers[4:6]
    steps_ref = refs.pop(0)
    queries_ref = refs.pop(0)
    row_ref = refs.pop(0)
    cell_ref = refs.pop(0)
    pieces = [refs.pop(0) for _ in range(piece_count)]
    if with_fresh:
        fresh_ref = refs.pop(0)
    if with_state:
        sum_in, stats_in = refs.pop(0), refs.pop(0)
    if last:
        (out,) = refs
    else:
        sum_ref, stats_ref = refs
    blocks = steps_ref.shape[0]
    each = queries_ref.shape[1] // blocks
    rows = ROW_BLOCKS * each
    width = keys_ref.shape[1]
    repeats = rows // HEAD_SIZE
    cached_slots = pieces[0].shape[0] // CHUNK
    nothing = cell_ref.shape[0] - 1

    @pl.loop(0, steps_ref[blocks - 1])
    def _(s):
        parts = [piece[pl.ds(s * CHUNK, CHUNK)] for piece in pieces]
        keys_ref[s] = jnp.concatenate([p[:, 0].reshape(-1, HEAD_SIZE) for p in parts], axis=0)
        values_ref[s] = jnp.concatenate([p[:, 1].reshape(-1, HEAD_SIZE) for p in parts], axis=0).T

    keys_ref[nothing] = jnp.zeros(keys_ref.shape[1:], keys_ref.dtype)
    values_ref[nothing] = jnp.zeros(values_ref.shape[1:], values_ref.dtype)
    if with_fresh:
        half = fresh_ref.shape[1] // 2
        per = width // half
        for f in range(blocks // per):
            part = fresh_ref[f * per : (f + 1) * per]
            keys_ref[cached_slots + f] = part[:, :half].reshape(width, HEAD_SIZE)
            values_ref[cached_slots + f] = part[:, half:].reshape(width, HEAD_SIZE).T
    if with_state:
        sum_ref[...] = sum_in[...]
        stats_ref[...] = stats_in[...]
    else:
        sum_ref[...] = jnp.zeros(sum_ref.shape, jnp.float32)
        line = lax.broadcasted_iota(jnp.int32, stats_ref.shape, 0)
        stats_ref[...] = jnp.where(line == 0, FIRST_PEAK, 0.0)

    total = jnp.int32(0)
    for block in range(blocks // ROW_BLOCKS):
        final = (block + 1) * ROW_BLOCKS - 1

        def add(s, total, block=block):
            pairs_ref[0, total] = block
            pairs_ref[1, total] = s
            return total + 1

        total = lax.fori_loop(0, steps_ref[final], add, total)
        if with_fresh:
            total = lax.fori_loop(cached_slots, cached_slots + final // per + 1, add, total)
    for n in range(2):
        pairs_ref[0, total + n] = 0
        pairs_ref[1, total + n] = nothing

    def place(block):
        return pl.ds(pl.multiple_of(block * rows, rows), rows)

    def score(t, side):
        mine, slot = place(pairs_ref[0, t]), pairs_ref[1, t]
        raw = jnp.dot(keys_ref[slot], queries_ref[:, mine], preferred_element_type=jnp.float32)
        usable = jnp.concatenate([cell_ref[slot]] * repeats, axis=1) < row_ref[:, mine]
        masked = jnp.where(usable, raw, MASKED_SCORE)
        scores[side][...] = masked
        peaks[side][...] = jnp.max(masked.reshape(width // 8, 8, rows), axis=0)

    def weigh(t, side):
        mine, slot = place(pairs_ref[0, t]), pairs_ref[1, t]
        old = stats_ref[0:1, mine]
        peak = jnp.maximum(old, jnp.max(peaks[side][...], axis=0, keepdims=True))
        weights = jnp.exp2((scores[side][...] - peak) * LOG2_SCALE)
        keep = jnp.exp2((old - peak) * LOG2_SCALE)
        mass = jnp.sum(weights.reshape(width // 8, 8, rows), axis=0)
        stats_ref[0:1, mine] = peak
        stats_ref[1:2, mine] = stats_ref[1:2, mine] * keep + jnp.sum(mass, axis=0, keepdims=True)
        sum_ref[:, mine] = sum_ref[:, mine] * keep + jnp.dot(
            values_ref[slot], weights.astype(jnp.bfloat16), preferred_element_type=jnp.float32
        )

    score(0, 0)

    @pl.loop(0, (total + 1) // 2)
    def _(u):
        score(2 * u + 1, 1)
        weigh(2 * u, 0)
        score(2 * u + 2, 0)
        weigh(2 * u + 1, 1)

    if last:
        for b in range(blocks):
            part = slice(b * each, (b + 1) * each)
            out[b, :HEAD_SIZE, :] = sum_ref[:, part]
            out[b, HEAD_SIZE:, :] = stats_ref[:, part]


def attend(steps, queries, row_pos, cells, pieces, fresh=None, state=None, last=False):
    blocks, rows = steps.shape[0], queries.shape[1]
    each = rows // blocks
    operands = [steps, queries, row_pos, cells, *pieces]
    if fresh is not None:
        operands.append(fresh)
    if state is not None:
        operands += list(state)
    in_specs = [pl.BlockSpec(memory_space=pltpu.VMEM)] * len(operands)
    in_specs[0] = pl.BlockSpec(memory_space=pltpu.SMEM)
    sums = [(HEAD_SIZE, rows), (8, rows)]
    out_shape = [(blocks, HEAD_SIZE + 8, each)] if last else sums
    slots, width = cells.shape[:2]
    tall = ROW_BLOCKS * each
    keys = slots * width
    return pl.pallas_call(
        functools.partial(attend_kernel, len(pieces), fresh is not None, state is not None, last),
        out_shape=[jax.ShapeDtypeStruct(shape, jnp.float32) for shape in out_shape],
        in_specs=in_specs,
        out_specs=[pl.BlockSpec(memory_space=pltpu.VMEM)] * len(out_shape),
        scratch_shapes=[
            pltpu.SMEM((2, slots * (rows // tall) + 2), jnp.int32),
            pltpu.VMEM((slots, width, HEAD_SIZE), jnp.bfloat16),
            pltpu.VMEM((slots, HEAD_SIZE, width), jnp.bfloat16),
            pltpu.VMEM((width, tall), jnp.float32),
            pltpu.VMEM((width, tall), jnp.float32),
            pltpu.VMEM((8, tall), jnp.float32),
            pltpu.VMEM((8, tall), jnp.float32),
        ]
        + [pltpu.VMEM(shape if last else (8, HEAD_SIZE), jnp.float32) for shape in sums],
        compiler_params=pltpu.CompilerParams(vmem_limit_bytes=VMEM_LIMIT),
        cost_estimate=pl.CostEstimate(
            flops=2 * 2 * rows * keys * HEAD_SIZE,
            bytes_accessed=8 * 1024 * 1024,
            transcendentals=rows * keys,
        ),
        name="attend",
    )(*operands)


def merge_kernel(parts_ref, out_ref):
    local = out_ref.shape[0]
    for h in range(parts_ref.shape[0] // HALVES):
        both = [parts_ref[h * HALVES + b] for b in range(HALVES)]
        peaks = [part[HEAD_SIZE : HEAD_SIZE + 1] for part in both]
        masses = [part[HEAD_SIZE + 1 : HEAD_SIZE + 2] for part in both]
        top = jnp.maximum(peaks[0], peaks[1])
        factors = [jnp.exp2((peak - top) * LOG2_SCALE) for peak in peaks]
        whole = factors[0] * masses[0] + factors[1] * masses[1]
        mixed = sum(
            part[:HEAD_SIZE] * (factor / whole) for part, factor in zip(both, factors)
        ).T.astype(out_ref.dtype)
        for g in range(GROUP):
            place = (h * GROUP + g) * HEAD_SIZE
            out_ref[:, place : place + HEAD_SIZE] = mixed[g * local : (g + 1) * local]


def merge(parts, local):
    heads = parts.shape[0] // HALVES
    return pl.pallas_call(
        merge_kernel,
        out_shape=jax.ShapeDtypeStruct((local, heads * GROUP * HEAD_SIZE), jnp.bfloat16),
        in_specs=[pl.BlockSpec(memory_space=pltpu.VMEM)],
        out_specs=pl.BlockSpec(memory_space=pltpu.VMEM),
        compiler_params=pltpu.CompilerParams(vmem_limit_bytes=VMEM_LIMIT),
        name="merge",
    )(parts)


def spread(column):
    return jnp.broadcast_to(column, column.shape[:-1] + (HEAD_SIZE,))


def shards(queries, fresh_kv, pool_key_values, holder_map, passage_lists, recompute):
    requests = lax.axis_size("req")
    members = lax.axis_size("ctx")
    me, member = lax.axis_index("req"), lax.axis_index("ctx")
    half = member % HALVES
    length = pool_key_values.shape[1]
    local = queries.shape[1]
    count = passage_lists.shape[1]
    span = length // (requests * HALVES)
    positions = recompute[0]

    pieces = cut(pool_key_values[0], requests)
    with jax.named_scope("scatter_pool"):
        pieces = lax.all_to_all(pieces, ("req", "ctx"), split_axis=0, concat_axis=0, tiled=True)
    with jax.named_scope("send_queries"):
        parts = address(queries[0], fresh_kv[0])
        parts = lax.all_to_all(parts, "ctx", split_axis=0, concat_axis=0, tiled=True)

    turn = jnp.arange(requests, dtype=jnp.int32) ^ me
    offsets = jnp.arange(span, dtype=jnp.int32)
    cells = (
        jnp.arange(count, dtype=jnp.int32)[None, :, None] * length
        + turn[:, None, None] * (length // requests)
        + half * span
        + offsets[None, None, :]
    )
    redone = jnp.any(cells[..., None] == positions, axis=-1)
    cells = jnp.where(redone, NEVER, cells).reshape(requests, count // CHUNK, CHUNK * span, 1)
    fresh_cells = positions.reshape(members, HALVES, local // HALVES) - 1
    fresh_cells = lax.dynamic_index_in_dim(fresh_cells, half, 1, keepdims=False)
    fresh_cells = fresh_cells.reshape(-1, len(TURNS[0]) * CHUNK * span, 1)
    row_pos = jnp.broadcast_to(positions.reshape(members, 1, local), (members, GROUP, local))
    row_pos = row_pos.reshape(1, -1)
    reach = CHUNK * length
    steps = (positions.reshape(members, local)[:, -1] + (reach - 1)) // reach

    wanted = holder_map[passage_lists][turn]
    picked = pick(wanted, pieces)
    with jax.named_scope("send_pieces"):
        arrived = {0: picked[0]}
        for d in (2, 3, 6, 7, 1):
            arrived[d] = swap(picked[d], "req", d)
        arrived[1], parts = lax.optimization_barrier((arrived[1], parts))
        arrived[1], *far = lax.optimization_barrier((arrived[1], picked[4], picked[5]))
        arrived[4], arrived[5] = swap(far[0], "req", 4), swap(far[1], "req", 5)

    own_queries, fresh = collect(parts, local)
    nothing = jnp.full((1,) + fresh_cells.shape[1:], NEVER, jnp.int32)
    state = None
    for n, group in enumerate(TURNS):
        place = [jnp.concatenate([cells[d] for d in group], axis=1)]
        if n == 0:
            place.append(fresh_cells)
        place.append(nothing[:, : place[0].shape[1]])
        state = attend(
            steps,
            own_queries,
            row_pos,
            spread(jnp.concatenate(place, axis=0)),
            [arrived[d] for d in group],
            fresh if n == 0 else None,
            state,
            n == len(TURNS) - 1,
        )
    with jax.named_scope("send_sums"):
        parts = lax.all_to_all(state[0], "ctx", split_axis=0, concat_axis=0, tiled=True)
    return merge(parts, local)[None]


def solution(mesh):
    in_specs = (
        P("req", "ctx", None),
        P("req", "ctx", None),
        P(("req", "ctx"), None, None),
        P(),
        P(),
        P("req", None),
    )
    out_specs = P("req", "ctx", None)
    return jax.shard_map(shards, mesh=mesh, in_specs=in_specs, out_specs=out_specs, check_vma=False)
```

```python
import functools

import jax
import jax.numpy as jnp
from jax import lax
from jax.experimental import pallas as pl
from jax.experimental.pallas import tpu as pltpu
from jax.sharding import PartitionSpec as P

KEY_VALUE_HEADS = 8
HEAD_SIZE = 128
GROUP = 4
HALVES = 2

MASKED_SCORE = -3e30
FIRST_PEAK = -1e30
NEVER = 1 << 30
LOG2_SCALE = 1.4426950408889634 / HEAD_SIZE**0.5
ROW_BLOCKS = 2
CHUNK = 4
TURNS = ((0, 1), (2, 3), (6, 7, 4, 5))
VMEM_LIMIT = 16 * 1024 * 1024


def cut_kernel(block_ref, out_ref, sem):
    for h in range(KEY_VALUE_HEADS):
        for which in range(2):
            column = (which * KEY_VALUE_HEADS + h) * HEAD_SIZE
            for b in range(HALVES):
                pltpu.make_async_copy(
                    block_ref.at[:, b, :, column : column + HEAD_SIZE],
                    out_ref.at[:, h, b, which],
                    sem,
                ).start()
    pltpu.make_async_copy(out_ref, out_ref, sem).wait()


def cut(block, requests):
    length, wide = block.shape
    span = length // (requests * HALVES)
    pieces = pl.pallas_call(
        cut_kernel,
        out_shape=jax.ShapeDtypeStruct(
            (requests, KEY_VALUE_HEADS, HALVES, 2, span, HEAD_SIZE), block.dtype
        ),
        in_specs=[pl.BlockSpec(memory_space=pl.ANY)],
        out_specs=pl.BlockSpec(memory_space=pl.ANY),
        scratch_shapes=[pltpu.SemaphoreType.DMA],
        compiler_params=pltpu.CompilerParams(vmem_limit_bytes=VMEM_LIMIT),
        name="cut",
    )(block.reshape(requests, HALVES, span, wide))
    return pieces.reshape(-1, 2, span, HEAD_SIZE)


def address_kernel(queries_ref, fresh_ref, out_ref):
    local = queries_ref.shape[0]
    part = local // HALVES
    rows = GROUP * local
    for h in range(KEY_VALUE_HEADS):
        for g in range(GROUP):
            column = (h * GROUP + g) * HEAD_SIZE
            tile = queries_ref[:, column : column + HEAD_SIZE]
            for b in range(HALVES):
                out_ref[h * HALVES + b, g * local : (g + 1) * local, :] = tile
        for which in range(2):
            column = (which * KEY_VALUE_HEADS + h) * HEAD_SIZE
            for b in range(HALVES):
                out_ref[h * HALVES + b, rows + which * part : rows + (which + 1) * part, :] = (
                    fresh_ref[b * part : (b + 1) * part, column : column + HEAD_SIZE]
                )


def address(queries, fresh):
    local = queries.shape[0]
    shape = (KEY_VALUE_HEADS * HALVES, (GROUP + 1) * local, HEAD_SIZE)
    return pl.pallas_call(
        address_kernel,
        out_shape=jax.ShapeDtypeStruct(shape, queries.dtype),
        in_specs=[pl.BlockSpec(memory_space=pltpu.VMEM)] * 2,
        out_specs=pl.BlockSpec(memory_space=pltpu.VMEM),
        name="address",
    )(queries, fresh)


def collect_kernel(parts_ref, queries_ref, fresh_ref):
    rows = parts_ref.shape[1] - fresh_ref.shape[1]
    for c in range(parts_ref.shape[0]):
        queries_ref[:, c * rows : (c + 1) * rows] = parts_ref[c, :rows, :].T
        fresh_ref[c] = parts_ref[c, rows:, :]


def collect(parts, local):
    count, tall = parts.shape[:2]
    rows = GROUP * local
    return pl.pallas_call(
        collect_kernel,
        out_shape=[
            jax.ShapeDtypeStruct((HEAD_SIZE, count * rows), parts.dtype),
            jax.ShapeDtypeStruct((count, tall - rows, HEAD_SIZE), parts.dtype),
        ],
        in_specs=[pl.BlockSpec(memory_space=pltpu.VMEM)],
        out_specs=[pl.BlockSpec(memory_space=pltpu.VMEM)] * 2,
        name="collect",
    )(parts)


def swap(pieces, axis, far):
    return lax.ppermute(pieces, axis, [(i, i ^ far) for i in range(lax.axis_size(axis))])


def pick_kernel(wanted_ref, pieces_ref, *rest):
    outs, sems = rest[:-1], rest[-1]
    count = outs[0].shape[0]
    for d, out in enumerate(outs):
        for j in range(count):
            slot = wanted_ref[d, j]
            pltpu.make_async_copy(pieces_ref.at[slot], out.at[j], sems.at[d]).start()
    for d, out in enumerate(outs):
        pltpu.make_async_copy(out, out, sems.at[d]).wait()


def pick(wanted, pieces):
    turns, count = wanted.shape
    shape = jax.ShapeDtypeStruct((count,) + pieces.shape[1:], pieces.dtype)
    return pl.pallas_call(
        pick_kernel,
        out_shape=[shape] * turns,
        in_specs=[
            pl.BlockSpec(memory_space=pltpu.SMEM),
            pl.BlockSpec(memory_space=pltpu.VMEM),
        ],
        out_specs=[pl.BlockSpec(memory_space=pl.ANY)] * turns,
        scratch_shapes=[pltpu.SemaphoreType.DMA((turns,))],
        compiler_params=pltpu.CompilerParams(vmem_limit_bytes=VMEM_LIMIT),
        cost_estimate=pl.CostEstimate(flops=0, bytes_accessed=2 * pieces.size * 2, transcendentals=0),
        name="pick",
    )(wanted, pieces)


def attend_kernel(piece_count, with_fresh, with_state, last, *refs):
    refs = list(refs)
    pairs_ref, keys_ref, values_ref, *buffers = refs[-9:]
    refs = refs[:-9]
    scores, peaks = buffers[0:2], buffers[2:4]
    if last:
        sum_ref, stats_ref = buffers[4:6]
    steps_ref = refs.pop(0)
    queries_ref = refs.pop(0)
    row_ref = refs.pop(0)
    cell_ref = refs.pop(0)
    pieces = [refs.pop(0) for _ in range(piece_count)]
    if with_fresh:
        fresh_ref = refs.pop(0)
    if with_state:
        sum_in, stats_in = refs.pop(0), refs.pop(0)
    if last:
        (out,) = refs
    else:
        sum_ref, stats_ref = refs
    blocks = steps_ref.shape[0]
    each = queries_ref.shape[1] // blocks
    rows = ROW_BLOCKS * each
    width = keys_ref.shape[1]
    repeats = rows // HEAD_SIZE
    chunk = width // (piece_count * pieces[0].shape[2])
    cached_slots = pieces[0].shape[0] // chunk
    nothing = cell_ref.shape[0] - 1

    @pl.loop(0, steps_ref[blocks - 1])
    def _(s):
        parts = [piece[pl.ds(s * chunk, chunk)] for piece in pieces]
        keys_ref[s] = jnp.concatenate([p[:, 0].reshape(-1, HEAD_SIZE) for p in parts], axis=0)
        values_ref[s] = jnp.concatenate([p[:, 1].reshape(-1, HEAD_SIZE) for p in parts], axis=0).T

    keys_ref[nothing] = jnp.zeros(keys_ref.shape[1:], keys_ref.dtype)
    values_ref[nothing] = jnp.zeros(values_ref.shape[1:], values_ref.dtype)
    if with_fresh:
        half = fresh_ref.shape[1] // 2
        per = width // half
        for f in range(blocks // per):
            part = fresh_ref[f * per : (f + 1) * per]
            keys_ref[cached_slots + f] = part[:, :half].reshape(width, HEAD_SIZE)
            values_ref[cached_slots + f] = part[:, half:].reshape(width, HEAD_SIZE).T
    if with_state:
        sum_ref[...] = sum_in[...]
        stats_ref[...] = stats_in[...]
    else:
        sum_ref[...] = jnp.zeros(sum_ref.shape, jnp.float32)
        line = lax.broadcasted_iota(jnp.int32, stats_ref.shape, 0)
        stats_ref[...] = jnp.where(line == 0, FIRST_PEAK, 0.0)

    total = jnp.int32(0)
    for block in range(blocks // ROW_BLOCKS):
        final = (block + 1) * ROW_BLOCKS - 1

        def add(s, total, block=block):
            pairs_ref[0, total] = block
            pairs_ref[1, total] = s
            return total + 1

        total = lax.fori_loop(0, steps_ref[final], add, total)
        if with_fresh:
            total = lax.fori_loop(cached_slots, cached_slots + final // per + 1, add, total)
    for n in range(2):
        pairs_ref[0, total + n] = 0
        pairs_ref[1, total + n] = nothing

    def place(block):
        return pl.ds(pl.multiple_of(block * rows, rows), rows)

    def score(t, side):
        mine, slot = place(pairs_ref[0, t]), pairs_ref[1, t]
        raw = jnp.dot(keys_ref[slot], queries_ref[:, mine], preferred_element_type=jnp.float32)
        usable = jnp.concatenate([cell_ref[slot]] * repeats, axis=1) < row_ref[:, mine]
        masked = jnp.where(usable, raw, MASKED_SCORE)
        scores[side][...] = masked
        peaks[side][...] = jnp.max(masked.reshape(width // 8, 8, rows), axis=0)

    def weigh(t, side):
        mine, slot = place(pairs_ref[0, t]), pairs_ref[1, t]
        old = stats_ref[0:1, mine]
        peak = jnp.maximum(old, jnp.max(peaks[side][...], axis=0, keepdims=True))
        weights = jnp.exp2((scores[side][...] - peak) * LOG2_SCALE)
        keep = jnp.exp2((old - peak) * LOG2_SCALE)
        mass = jnp.sum(weights.reshape(width // 8, 8, rows), axis=0)
        stats_ref[0:1, mine] = peak
        stats_ref[1:2, mine] = stats_ref[1:2, mine] * keep + jnp.sum(mass, axis=0, keepdims=True)
        sum_ref[:, mine] = sum_ref[:, mine] * keep + jnp.dot(
            values_ref[slot], weights.astype(jnp.bfloat16), preferred_element_type=jnp.float32
        )

    score(0, 0)

    @pl.loop(0, (total + 1) // 2)
    def _(u):
        score(2 * u + 1, 1)
        weigh(2 * u, 0)
        score(2 * u + 2, 0)
        weigh(2 * u + 1, 1)

    if last:
        for b in range(blocks):
            part = slice(b * each, (b + 1) * each)
            out[b, :HEAD_SIZE, :] = sum_ref[:, part]
            out[b, HEAD_SIZE:, :] = stats_ref[:, part]


def attend(steps, queries, row_pos, cells, pieces, fresh=None, state=None, last=False):
    blocks, rows = steps.shape[0], queries.shape[1]
    each = rows // blocks
    operands = [steps, queries, row_pos, cells, *pieces]
    if fresh is not None:
        operands.append(fresh)
    if state is not None:
        operands += list(state)
    in_specs = [pl.BlockSpec(memory_space=pltpu.VMEM)] * len(operands)
    in_specs[0] = pl.BlockSpec(memory_space=pltpu.SMEM)
    sums = [(HEAD_SIZE, rows), (8, rows)]
    out_shape = [(blocks, HEAD_SIZE + 8, each)] if last else sums
    slots, width = cells.shape[:2]
    tall = ROW_BLOCKS * each
    keys = slots * width
    return pl.pallas_call(
        functools.partial(attend_kernel, len(pieces), fresh is not None, state is not None, last),
        out_shape=[jax.ShapeDtypeStruct(shape, jnp.float32) for shape in out_shape],
        in_specs=in_specs,
        out_specs=[pl.BlockSpec(memory_space=pltpu.VMEM)] * len(out_shape),
        scratch_shapes=[
            pltpu.SMEM((2, slots * (rows // tall) + 2), jnp.int32),
            pltpu.VMEM((slots, width, HEAD_SIZE), jnp.bfloat16),
            pltpu.VMEM((slots, HEAD_SIZE, width), jnp.bfloat16),
            pltpu.VMEM((width, tall), jnp.float32),
            pltpu.VMEM((width, tall), jnp.float32),
            pltpu.VMEM((8, tall), jnp.float32),
            pltpu.VMEM((8, tall), jnp.float32),
        ]
        + [pltpu.VMEM(shape if last else (8, HEAD_SIZE), jnp.float32) for shape in sums],
        compiler_params=pltpu.CompilerParams(vmem_limit_bytes=VMEM_LIMIT),
        cost_estimate=pl.CostEstimate(
            flops=2 * 2 * rows * keys * HEAD_SIZE,
            bytes_accessed=8 * 1024 * 1024,
            transcendentals=rows * keys,
        ),
        name="attend",
    )(*operands)


def merge_kernel(parts_ref, out_ref):
    local = out_ref.shape[0]
    for h in range(parts_ref.shape[0] // HALVES):
        both = [parts_ref[h * HALVES + b] for b in range(HALVES)]
        peaks = [part[HEAD_SIZE : HEAD_SIZE + 1] for part in both]
        masses = [part[HEAD_SIZE + 1 : HEAD_SIZE + 2] for part in both]
        top = jnp.maximum(peaks[0], peaks[1])
        factors = [jnp.exp2((peak - top) * LOG2_SCALE) for peak in peaks]
        whole = factors[0] * masses[0] + factors[1] * masses[1]
        mixed = sum(
            part[:HEAD_SIZE] * (factor / whole) for part, factor in zip(both, factors)
        ).T.astype(out_ref.dtype)
        for g in range(GROUP):
            place = (h * GROUP + g) * HEAD_SIZE
            out_ref[:, place : place + HEAD_SIZE] = mixed[g * local : (g + 1) * local]


def merge(parts, local):
    heads = parts.shape[0] // HALVES
    return pl.pallas_call(
        merge_kernel,
        out_shape=jax.ShapeDtypeStruct((local, heads * GROUP * HEAD_SIZE), jnp.bfloat16),
        in_specs=[pl.BlockSpec(memory_space=pltpu.VMEM)],
        out_specs=pl.BlockSpec(memory_space=pltpu.VMEM),
        compiler_params=pltpu.CompilerParams(vmem_limit_bytes=VMEM_LIMIT),
        name="merge",
    )(parts)


def spread(column):
    return jnp.broadcast_to(column, column.shape[:-1] + (HEAD_SIZE,))


def shards(queries, fresh_kv, pool_key_values, holder_map, passage_lists, recompute):
    requests = lax.axis_size("req")
    members = lax.axis_size("ctx")
    me, member = lax.axis_index("req"), lax.axis_index("ctx")
    half = member % HALVES
    length = pool_key_values.shape[1]
    local = queries.shape[1]
    count = passage_lists.shape[1]
    span = length // (requests * HALVES)
    positions = recompute[0]

    pieces = cut(pool_key_values[0], requests)
    with jax.named_scope("scatter_pool"):
        pieces = lax.all_to_all(pieces, ("req", "ctx"), split_axis=0, concat_axis=0, tiled=True)
    with jax.named_scope("send_queries"):
        parts = address(queries[0], fresh_kv[0])
        parts = lax.all_to_all(parts, "ctx", split_axis=0, concat_axis=0, tiled=True)

    turn = jnp.arange(requests, dtype=jnp.int32) ^ me
    offsets = jnp.arange(span, dtype=jnp.int32)
    cells = (
        jnp.arange(count, dtype=jnp.int32)[None, :, None] * length
        + turn[:, None, None] * (length // requests)
        + half * span
        + offsets[None, None, :]
    )
    redone = jnp.any(cells[..., None] == positions, axis=-1)
    cells = jnp.where(redone, NEVER, cells)
    fresh_cells = positions.reshape(members, HALVES, local // HALVES) - 1
    fresh_cells = lax.dynamic_index_in_dim(fresh_cells, half, 1, keepdims=False)
    fresh_cells = fresh_cells.reshape(-1, len(TURNS[0]) * CHUNK * span, 1)
    row_pos = jnp.broadcast_to(positions.reshape(members, 1, local), (members, GROUP, local))
    row_pos = row_pos.reshape(1, -1)
    wanted = holder_map[passage_lists][turn]
    picked = pick(wanted, pieces)
    with jax.named_scope("send_pieces"):
        arrived = {0: picked[0]}
        for d in (2, 3, 6, 7, 1):
            arrived[d] = swap(picked[d], "req", d)
        arrived[1], parts = lax.optimization_barrier((arrived[1], parts))
        arrived[1], *far = lax.optimization_barrier((arrived[1], picked[4], picked[5]))
        arrived[4], arrived[5] = swap(far[0], "req", 4), swap(far[1], "req", 5)

    own_queries, fresh = collect(parts, local)
    nothing = jnp.full((1,) + fresh_cells.shape[1:], NEVER, jnp.int32)
    state = None
    for n, group in enumerate(TURNS):
        chunk = CHUNK * 2 // len(group)
        steps = (positions.reshape(members, local)[:, -1] + (chunk * length - 1)) // (chunk * length)
        place = [cells[d].reshape(count // chunk, chunk * span, 1) for d in group]
        place = [jnp.concatenate(place, axis=1)]
        if n == 0:
            place.append(fresh_cells)
        place.append(nothing[:, : place[0].shape[1]])
        state = attend(
            steps,
            own_queries,
            row_pos,
            spread(jnp.concatenate(place, axis=0)),
            [arrived[d] for d in group],
            fresh if n == 0 else None,
            state,
            n == len(TURNS) - 1,
        )
    with jax.named_scope("send_sums"):
        parts = lax.all_to_all(state[0], "ctx", split_axis=0, concat_axis=0, tiled=True)
    return merge(parts, local)[None]


def solution(mesh):
    in_specs = (
        P("req", "ctx", None),
        P("req", "ctx", None),
        P(("req", "ctx"), None, None),
        P(),
        P(),
        P("req", None),
    )
    out_specs = P("req", "ctx", None)
    return jax.shard_map(shards, mesh=mesh, in_specs=in_specs, out_specs=out_specs, check_vma=False)
```
